256 devices in a mesh: tok: 4 (over x), feat: 64 (over y, z, core).
Axes of the slice: x: 4, y: 4, z: 8, core: 2. Of those that a mesh axis runs over, the one named last changes fastest.
Arguments:
- activations: bfloat16 [32768, 28672], P('tok', 'feat'), may hold values from -6 to 6
- labels: int32 [8, 32768], P(None, 'tok'), may hold values 0 or 1
- probe_weights: bfloat16 [8, 28672], P(None, 'feat'), may hold values from -0.25 to 0.25
- direction: bfloat16 [8, 28672], P(None, 'feat'), may hold values from -0.25 to 0.25
- group_ids: int32 [28672], P('feat'), may hold values from 0 to 63, never falling along the last dimension, each value on 1 to 896 neighbouring positions
Outputs:
- gradient: float32 [8, 28672], P(None, 'feat')
- hess_vec: float32 [8, 28672], P(None, 'feat')
The draws below stay inside these ranges and needn't reach their ends.
Inputs may be any that keep to these rules, and one draw needn't show every extreme that they name: `group_ids`: group numbers never fall along the neurons; every group holds 1 to 896 neurons in a row, some group exactly that many.
All inputs are finite; a program needn't handle non-finite values. No bound on the sum of `labels` on one device may be relied on, other than what follows from the above.
Results may differ from the reference program's by a relative error of at most 0.0022.
Values may be sent and summed in bfloat16 or wider, within the bound.
No kernel may reach another device: no remote copies, remote signals or barrier semaphores. Data moves between devices by JAX's collectives and lax.ppermute only.
A program may use at most 64 MiB of HBM per device.

```python
import math
import jax
import jax.numpy as jnp
import numpy as np
from jax import lax

NEURONS = 28672
PROBES = 8
GROUPS = 64
TOKENS = 32768


def common_normal(key):
    return jnp.clip(jax.random.normal(key, (PROBES, NEURONS), jnp.float32), -6.0, 6.0)


def draw_probe_weights(key, part):
    shared = common_normal(key)
    spread = math.log(10.0)
    key = jax.random.fold_in(key, 11)
    first, second = jax.random.split(key, 2)
    rows = jnp.exp(jax.random.uniform(first, (1, NEURONS), jnp.float32, 0.0, spread))
    cols = jnp.exp(jax.random.uniform(second, (PROBES, 1), jnp.float32, 0.0, math.log(10.0)))
    values = jnp.clip(shared * rows * cols * (0.068 / math.sqrt(NEURONS)), -0.25, 0.25)
    return values.astype(jnp.bfloat16)


def draw_direction(key, part):
    shared = common_normal(key)
    key = jax.random.fold_in(key, 23)
    first, second, third = jax.random.split(key, 3)
    spread = math.log(10.0)
    own = jnp.clip(jax.random.normal(third, (PROBES, NEURONS), jnp.float32), -6.0, 6.0)
    rows = jnp.exp(jax.random.uniform(first, (1, NEURONS), jnp.float32, 0.0, spread))
    cols = jnp.exp(jax.random.uniform(second, (PROBES, 1), jnp.float32, 0.0, math.log(10.0)))
    mixed = 0.6 * shared + 0.8 * own
    values = jnp.clip(mixed * rows * cols * (0.068 / math.sqrt(NEURONS)), -0.25, 0.25)
    return values.astype(jnp.bfloat16)


def set_ends(drawn, own_key, low, high):
    spot = [jax.random.randint(jax.random.fold_in(own_key, axis), (), 0, length) for axis, length in enumerate(drawn.shape)]
    widest = drawn.shape.index(max(drawn.shape))
    neighbour = spot[:widest] + [(spot[widest] + 1) % drawn.shape[widest]] + spot[widest + 1:]
    return drawn.at[tuple(spot)].set(low).at[tuple(neighbour)].set(high)


def level_of(stream_key, extent, cuts, low, high):
    gain = 1.0
    for position, shards_of in cuts:
        heights = jax.random.uniform(jax.random.fold_in(jax.random.fold_in(stream_key, 6), position), (shards_of,), jnp.float32, low / len(cuts), high / len(cuts))
        gain = gain * jnp.repeat(jnp.exp(heights), extent[position] // shards_of).reshape((-1,) + (1,) * (len(extent) - 1 - position))
    return gain


def split_up(amount, total, bound, slope):
    weights = [(1 << 20) // math.isqrt(grade ** slope) + 1 for grade in range(2, amount + 1)]
    rest, counts = total - bound - (amount - 1), [1] * (amount - 1)
    while rest > 0:
        movable = [i for i in range(amount - 1) if counts[i] < bound]
        pool, remaining = sum([weights[i] for i in movable]), rest
        for i in movable:
            more = min(bound - counts[i], max(1, remaining * weights[i] // pool), rest)
            counts[i] = counts[i] + more
            rest = rest - more
    return np.array([bound] + counts)


def uneven_parts(key, number_of, total, limit, slope):
    if number_of == 2:
        one = jax.random.randint(key, (), max(1, total - limit), min(limit, total - 1) + 1)
        return jnp.stack([one, total - one])
    lengths = jnp.asarray(split_up(number_of, total, limit, slope), jnp.int32)
    couples = (number_of - 1) // 2
    giver, taker = lengths[1:1 + 2 * couples:2], lengths[2:2 + 2 * couples:2]
    room = jnp.minimum(giver - 1, limit - taker)
    passed = jax.random.randint(jax.random.fold_in(key, 1), (couples,), 0, 1 << 20) % (room + 1)
    lengths = lengths.at[1:1 + 2 * couples:2].set(giver - passed).at[2:2 + 2 * couples:2].set(taker + passed)
    return lengths[jax.random.permutation(jax.random.fold_in(key, 2), number_of)]


def noise(key, extent, width, most, cuts=(), dtype=jnp.bfloat16):
    entries = width * jax.random.normal(key, extent, jnp.float32)
    if cuts:
        entries = entries * level_of(key, extent, cuts, -0.22, 0.18)
    return jnp.clip(entries, -most, most).astype(dtype)


def setup_inputs(seed: int = 0) -> dict:
    arg_keys = jax.random.split(jax.random.key(seed), 6)
    activations = noise(arg_keys[0], (TOKENS, NEURONS), 1.0, 6.0, ((0, 4), (1, 64)))
    labels = set_ends((jax.random.randint(arg_keys[1], (PROBES, TOKENS), 0, 2) < 1).astype(jnp.int32), jax.random.fold_in(arg_keys[1], 1), 0, 1)
    probe_weights = draw_probe_weights(jax.random.fold_in(arg_keys[5], 71), 0)
    direction = draw_direction(jax.random.fold_in(arg_keys[5], 71), 0)
    group_ids = jnp.searchsorted(jnp.cumsum(uneven_parts(arg_keys[4], GROUPS, NEURONS, 2 * NEURONS // GROUPS, 0)), jnp.arange(NEURONS), side="right").astype(jnp.int32)
    return dict(activations=activations, labels=labels, probe_weights=probe_weights, direction=direction, group_ids=group_ids)


DELTA = 0.05
LAMBDA_WEIGHT = 8.0

def reference(activations, labels, probe_weights, direction, group_ids):
    stacked = jnp.concatenate([probe_weights, direction], 0)
    margins = lax.dot_general(stacked, activations, (((1,), (1,)), ((), ())), preferred_element_type=jnp.float32)
    logits = margins[:PROBES]
    slopes = margins[PROBES:]
    likely = jax.nn.sigmoid(logits)
    weighted = jnp.concatenate([likely - labels.astype(jnp.float32), likely * (1.0 - likely) * slopes], 0).astype(jnp.bfloat16)
    fitted = jnp.dot(weighted, activations, preferred_element_type=jnp.float32) / math.sqrt(TOKENS)
    wide_weights = probe_weights.astype(jnp.float32)
    wide_direction = direction.astype(jnp.float32)
    products = jnp.concatenate([wide_weights * wide_weights, wide_weights * wide_direction], 0)
    totals = jax.ops.segment_sum(products.T, group_ids, num_segments=GROUPS).T
    group_norm = jnp.sqrt(totals[:PROBES] + DELTA * DELTA)
    scale = group_norm[:, group_ids]
    cross = totals[PROBES:][:, group_ids]
    gradient = fitted[:PROBES] + LAMBDA_WEIGHT * wide_weights / scale
    hess_vec = fitted[PROBES:] + LAMBDA_WEIGHT * (wide_direction / scale - wide_weights * cross / (scale * scale * scale))
    return (gradient, hess_vec)
```

```python
import math

import jax
import jax.numpy as jnp
from jax import lax
from jax.sharding import PartitionSpec as P

GROUPS = 64


DELTA = 0.05
LAMBDA_WEIGHT = 8.0


def local(activations, labels, probe_weights, direction, group_ids):
    probes = probe_weights.shape[0]
    rows = 2 * probes
    tokens = activations.shape[0]
    planes = lax.axis_size("tok")
    devices = lax.axis_size("feat")
    chips = devices // 2
    share = tokens // chips
    chip = lax.axis_index("feat") // 2
    by_core = [[2 * i + core for i in range(chips)] for core in range(2)]
    swap = [(i, i ^ 1) for i in range(devices)]

    stacked = jnp.concatenate([probe_weights, direction], 0)
    partial_value = lax.dot_general(
        stacked, activations, (((1,), (1,)), ((), ())), preferred_element_type=jnp.float32
    )
    wide_weights = probe_weights.astype(jnp.float32)
    wide_direction = direction.astype(jnp.float32)
    member = (group_ids[None, :] == jnp.arange(GROUPS, dtype=jnp.int32)[:, None]).astype(
        jnp.float32
    )
    products = jnp.concatenate([wide_weights * wide_weights, wide_weights * wide_direction], 0)
    local_stats = lax.dot_general(
        products,
        member,
        (((1,), (1,)), ((), ())),
        precision=lax.Precision.HIGHEST,
        preferred_element_type=jnp.float32,
    )
    high = lax.reduce_precision(local_stats, 8, 7)
    split_stats = jnp.concatenate([high, local_stats - high], 1).astype(jnp.bfloat16)

    outgoing = jnp.concatenate(
        [
            partial_value.reshape(rows, chips, share).transpose(1, 0, 2).astype(jnp.bfloat16),
            jnp.broadcast_to(split_stats[None], (chips, rows, 2 * GROUPS)),
        ],
        2,
    )
    arrived = lax.all_to_all(outgoing, "feat", 0, 0, axis_index_groups=by_core)
    summed = arrived.astype(jnp.float32).sum(0)
    summed = summed + lax.ppermute(summed, "feat", swap)
    margins = summed[:, :share]
    totals = summed[:, share : share + GROUPS] + summed[:, share + GROUPS :]

    targets = lax.dynamic_slice_in_dim(labels, chip * share, share, 1)
    likely = jax.nn.sigmoid(margins[:probes])
    weighted = jnp.concatenate(
        [likely - targets.astype(jnp.float32), likely * (1.0 - likely) * margins[probes:]], 0
    ).astype(jnp.bfloat16)
    copies = jnp.broadcast_to(weighted[None], (chips, rows, share))
    gathered = lax.all_to_all(copies, "feat", 0, 0, axis_index_groups=by_core)
    weighted_all = gathered.transpose(1, 0, 2).reshape(rows, tokens)

    local_fit = jnp.dot(weighted_all, activations, preferred_element_type=jnp.float32)
    one, two, three = (
        lax.ppermute(local_fit, "tok", [(i, (i + hop) % planes) for i in range(planes)])
        for hop in (1, 2, 3)
    )
    fitted = (local_fit + two) + (one + three)
    fitted = fitted / math.sqrt(tokens * planes)

    group_norm = jnp.sqrt(totals[:probes] + DELTA * DELTA)
    spread = jnp.dot(
        jnp.concatenate([group_norm, totals[probes:]], 0),
        member,
        precision=lax.Precision.HIGHEST,
        preferred_element_type=jnp.float32,
    )
    scale = spread[:probes]
    cross = spread[probes:]
    gradient = fitted[:probes] + LAMBDA_WEIGHT * wide_weights / scale
    hess_vec = fitted[probes:] + LAMBDA_WEIGHT * (
        wide_direction / scale - wide_weights * cross / (scale * scale * scale)
    )
    return (gradient, hess_vec)


def solution(mesh):
    return jax.shard_map(
        local,
        mesh=mesh,
        in_specs=(P("tok", "feat"), P(None, "tok"), P(None, "feat"), P(None, "feat"), P("feat")),
        out_specs=(P(None, "feat"), P(None, "feat")),
        check_vma=False,
    )
```

```python
import math

import jax
import jax.numpy as jnp
from jax import lax
from jax.experimental import pallas as pl
from jax.experimental.pallas import tpu as pltpu
from jax.sharding import PartitionSpec as P

GROUPS = 64


DELTA = 0.05
LAMBDA_WEIGHT = 8.0

LANES = 128
PIECES = 4


def transposed_dot(left, right, precision=None):
    return lax.dot_general(
        left,
        right,
        (((1,), (1,)), ((), ())),
        precision=precision,
        preferred_element_type=jnp.float32,
    )


def margins_kernel(
    w_ref, d_ref, g_ref, labels_ref, a_ref,
    mine, theirs, stats_mine, stats_theirs, targets,
    a_mine, a_theirs, labels_sem, a_sems,
):
    me = lax.axis_index("feat")
    core, chip = lax.rem(me, 2), lax.div(me, 2)
    half = a_mine.shape[1]
    piece = half // PIECES
    copies = []
    for side, held in ((1 - core, a_theirs), (core, a_mine)):
        for i in range(PIECES):
            start = pl.multiple_of(side * half + i * piece, LANES)
            copy = pltpu.make_async_copy(
                a_ref.at[:, pl.ds(start, piece)],
                held.at[:, pl.ds(i * piece, piece)],
                a_sems.at[len(copies)],
            )
            copy.start()
            copies.append(copy)
    share = targets.shape[1]
    spot = pl.multiple_of(core * half + chip * share, LANES)
    labels_copy = pltpu.make_async_copy(labels_ref.at[:, pl.ds(spot, share)], targets, labels_sem)
    labels_copy.start()

    wide_weights = w_ref[...].astype(jnp.float32)
    wide_direction = d_ref[...].astype(jnp.float32)
    number = lax.broadcasted_iota(jnp.int32, (GROUPS, g_ref.shape[1]), 0)
    member = (number == g_ref[...]).astype(jnp.float32)
    squares = transposed_dot(wide_weights * wide_weights, member, lax.Precision.HIGHEST)
    crosses = transposed_dot(wide_weights * wide_direction, member, lax.Precision.HIGHEST)
    stats_mine[...] = jnp.where(core == 0, squares, crosses)
    stats_theirs[...] = jnp.where(core == 0, crosses, squares)

    stacked = jnp.concatenate([w_ref[...], d_ref[...]], 0)
    per_piece = piece // LANES
    for n, copy in enumerate(copies):
        copy.wait()
        held, out = (a_theirs, theirs) if n < PIECES else (a_mine, mine)
        i = n % PIECES
        product = jnp.dot(
            stacked, held[:, i * piece : (i + 1) * piece], preferred_element_type=jnp.float32
        )
        for k in range(per_piece):
            out[i * per_piece + k] = product[:, k * LANES : (k + 1) * LANES]
    labels_copy.wait()


def weighted_kernel(arrived, targets, copies, totals):
    rows = copies.shape[1]
    probes = rows // 2
    summed = jnp.sum(arrived[...].astype(jnp.float32), 0)
    logits, slopes, split_stats = summed[:probes], summed[probes:rows], summed[rows:]
    likely = 1.0 / (1.0 + jnp.exp(-logits))
    weighted = jnp.concatenate(
        [likely - targets[...].astype(jnp.float32), likely * (1.0 - likely) * slopes], 0
    ).astype(jnp.bfloat16)
    copies[...] = jnp.broadcast_to(weighted[None], copies.shape)
    totals[...] = split_stats[:, :GROUPS] + split_stats[:, GROUPS:]


def flatten(weighted, flat):
    for k in range(weighted.shape[0]):
        flat[:, k * LANES : (k + 1) * LANES] = weighted[k]


def fit_mine_kernel(weighted, a_ref, out, a_theirs, flat, a_mine, sems):
    core = lax.rem(lax.axis_index("feat"), 2)
    half = a_mine.shape[1]
    piece = half // PIECES
    copies = []
    for side, held in ((core, a_mine), (1 - core, a_theirs)):
        for i in range(PIECES):
            start = pl.multiple_of(side * half + i * piece, LANES)
            copy = pltpu.make_async_copy(
                a_ref.at[:, pl.ds(start, piece)],
                held.at[:, pl.ds(i * piece, piece)],
                sems.at[len(copies)],
            )
            copy.start()
            copies.append(copy)
    flatten(weighted, flat)
    total = jnp.zeros(out.shape, jnp.float32)
    for i in range(PIECES):
        copies[i].wait()
        at = slice(i * piece, (i + 1) * piece)
        total = total + transposed_dot(flat[:, at], a_mine[:, at])
    out[...] = total
    for copy in copies[PIECES:]:
        copy.wait()


def fit_theirs_kernel(weighted, a_theirs, base, out, flat):
    flatten(weighted, flat)
    out[...] = base[...] + transposed_dot(flat[...], a_theirs[...])


def local(activations, labels, probe_weights, direction, group_ids):
    probes, width = probe_weights.shape
    rows = 2 * probes
    tokens = activations.shape[0]
    half = tokens // 2
    planes = lax.axis_size("tok")
    devices = lax.axis_size("feat")
    chips = devices // 2
    share = half // chips
    core = lax.rem(lax.axis_index("feat"), 2)
    by_core = [[2 * i + side for i in range(chips)] for side in range(2)]
    swap = [(i, i ^ 1) for i in range(devices)]
    f32, bf16 = jnp.float32, jnp.bfloat16
    vmem, hbm = pl.BlockSpec(memory_space=pltpu.VMEM), pl.BlockSpec(memory_space=pltpu.HBM)

    by_neuron = pltpu.with_memory_space_constraint(activations.T, pltpu.HBM)
    mine, theirs, stats_mine, stats_theirs, targets = pl.pallas_call(
        margins_kernel,
        out_shape=[
            jax.ShapeDtypeStruct((chips, rows, share), f32),
            jax.ShapeDtypeStruct((chips, rows, share), f32),
            jax.ShapeDtypeStruct((probes, GROUPS), f32),
            jax.ShapeDtypeStruct((probes, GROUPS), f32),
            jax.ShapeDtypeStruct((probes, share), jnp.int32),
        ],
        in_specs=[vmem, vmem, vmem, hbm, hbm],
        out_specs=[vmem] * 5,
        scratch_shapes=[
            pltpu.VMEM((width, half), bf16),
            pltpu.VMEM((width, half), bf16),
            pltpu.SemaphoreType.DMA,
            pltpu.SemaphoreType.DMA((2 * PIECES,)),
        ],
        compiler_params=pltpu.CompilerParams(vmem_limit_bytes=24 << 20),
        name="margins",
    )(probe_weights, direction, group_ids[None, :], pltpu.with_memory_space_constraint(labels, pltpu.HBM), by_neuron)

    stats = stats_mine + lax.ppermute(stats_theirs, "feat", swap)
    high = lax.reduce_precision(stats, 8, 7)
    split_stats = jnp.concatenate([high, stats - high], 1).astype(bf16)
    pair_sum = (mine + lax.ppermute(theirs, "feat", swap)).astype(bf16)
    outgoing = jnp.concatenate(
        [pair_sum, jnp.broadcast_to(split_stats[None], (chips, probes, 2 * GROUPS))], 1
    )
    arrived = lax.all_to_all(outgoing, "feat", 0, 0, axis_index_groups=by_core)
    copies, totals_mine = pl.pallas_call(
        weighted_kernel,
        out_shape=[
            jax.ShapeDtypeStruct((chips, rows, share), bf16),
            jax.ShapeDtypeStruct((probes, GROUPS), f32),
        ],
        in_specs=[vmem] * 2,
        out_specs=[vmem] * 2,
        compiler_params=pltpu.CompilerParams(vmem_limit_bytes=4 << 20),
        name="weighted",
    )(arrived, targets)
    weighted_mine = lax.all_to_all(copies, "feat", 0, 0, axis_index_groups=by_core)
    weighted_theirs = lax.ppermute(weighted_mine, "feat", swap)

    half_cost = pl.CostEstimate(
        flops=2 * rows * width * half, bytes_accessed=4 * width * half, transcendentals=0
    )
    fit_mine, a_theirs = pl.pallas_call(
        fit_mine_kernel,
        out_shape=[jax.ShapeDtypeStruct((rows, width), f32), pltpu.VMEM((width, half), bf16)],
        in_specs=[vmem, hbm],
        out_specs=[vmem] * 2,
        scratch_shapes=[
            pltpu.VMEM((rows, half), bf16),
            pltpu.VMEM((width, half), bf16),
            pltpu.SemaphoreType.DMA((2 * PIECES,)),
        ],
        compiler_params=pltpu.CompilerParams(vmem_limit_bytes=24 << 20),
        cost_estimate=half_cost,
        name="fit_mine",
    )(weighted_mine, by_neuron)
    fit_mine, totals_mine = lax.optimization_barrier((fit_mine, totals_mine))
    local_fit = pl.pallas_call(
        fit_theirs_kernel,
        out_shape=jax.ShapeDtypeStruct((rows, width), f32),
        in_specs=[vmem] * 3,
        out_specs=vmem,
        scratch_shapes=[pltpu.VMEM((rows, half), bf16)],
        compiler_params=pltpu.CompilerParams(vmem_limit_bytes=8 << 20),
        cost_estimate=half_cost,
        name="fit_theirs",
    )(weighted_theirs, pltpu.with_memory_space_constraint(a_theirs, pltpu.VMEM), fit_mine)
    one, two, three = (
        lax.ppermute(local_fit, "tok", [(i, (i + hop) % planes) for i in range(planes)])
        for hop in (1, 2, 3)
    )
    fitted = (local_fit + two) + (one + three)
    fitted = fitted / math.sqrt(tokens * planes)

    totals_theirs = lax.ppermute(totals_mine, "feat", swap)
    squares = jnp.where(core == 0, totals_mine, totals_theirs)
    crosses = jnp.where(core == 0, totals_theirs, totals_mine)
    wide_weights = probe_weights.astype(f32)
    wide_direction = direction.astype(f32)
    member = (group_ids[None, :] == jnp.arange(GROUPS, dtype=jnp.int32)[:, None]).astype(f32)
    group_norm = jnp.sqrt(squares + DELTA * DELTA)
    spread = jnp.dot(
        jnp.concatenate([group_norm, crosses], 0),
        member,
        precision=lax.Precision.HIGHEST,
        preferred_element_type=f32,
    )
    scale = spread[:probes]
    cross = spread[probes:]
    gradient = fitted[:probes] + LAMBDA_WEIGHT * wide_weights / scale
    hess_vec = fitted[probes:] + LAMBDA_WEIGHT * (
        wide_direction / scale - wide_weights * cross / (scale * scale * scale)
    )
    return (gradient, hess_vec)


def solution(mesh):
    return jax.shard_map(
        local,
        mesh=mesh,
        in_specs=(P("tok", "feat"), P(None, "tok"), P(None, "feat"), P(None, "feat"), P("feat")),
        out_specs=(P(None, "feat"), P(None, "feat")),
        check_vma=False,
    )
```

```python
import math

import jax
import jax.numpy as jnp
from jax import lax
from jax.experimental import pallas as pl
from jax.experimental.pallas import tpu as pltpu
from jax.sharding import PartitionSpec as P

GROUPS = 64


DELTA = 0.05
LAMBDA_WEIGHT = 8.0

LANES = 128
PIECES = 4


def transposed_dot(left, right, precision=None):
    return lax.dot_general(
        left,
        right,
        (((1,), (1,)), ((), ())),
        precision=precision,
        preferred_element_type=jnp.float32,
    )


def start_half(a_ref, side, held, sems):
    half = held.shape[1]
    piece = half // PIECES
    copies = []
    for i in range(PIECES):
        start = pl.multiple_of(side * half + i * piece, LANES)
        copy = pltpu.make_async_copy(
            a_ref.at[:, pl.ds(start, piece)], held.at[:, pl.ds(i * piece, piece)], sems.at[i]
        )
        copy.start()
        copies.append(copy)
    return copies


def multiply_half(stacked, copies, held, out):
    piece = held.shape[1] // PIECES
    per_piece = piece // LANES
    for i, copy in enumerate(copies):
        copy.wait()
        product = jnp.dot(
            stacked, held[:, i * piece : (i + 1) * piece], preferred_element_type=jnp.float32
        )
        for k in range(per_piece):
            out[i * per_piece + k] = product[:, k * LANES : (k + 1) * LANES]


def margins_theirs_kernel(
    w_ref, d_ref, g_ref, a_ref, theirs, stacked_out, ids_out, w, d, held, small_sems, a_sems
):
    core = lax.rem(lax.axis_index("feat"), 2)
    small = [
        pltpu.make_async_copy(source, target, small_sems.at[i])
        for i, (source, target) in enumerate(((w_ref, w), (d_ref, d), (g_ref, ids_out)))
    ]
    for copy in small:
        copy.start()
    copies = start_half(a_ref, 1 - core, held, a_sems)
    for copy in small:
        copy.wait()
    stacked = jnp.concatenate([w[...], d[...]], 0)
    stacked_out[...] = stacked
    wide_weights = w[...].astype(jnp.float32)
    products = jnp.concatenate(
        [wide_weights * wide_weights, wide_weights * d[...].astype(jnp.float32)], 0
    )
    number = lax.broadcasted_iota(jnp.int32, (LANES, ids_out.shape[1]), 0)
    member = (number == ids_out[...]).astype(jnp.float32)
    theirs[theirs.shape[0] - 1] = transposed_dot(products, member, lax.Precision.HIGHEST)
    multiply_half(stacked, copies, held, theirs)


def margins_mine_kernel(stacked, labels_ref, a_ref, mine, targets, held, labels_sem, a_sems):
    me = lax.axis_index("feat")
    core, chip = lax.rem(me, 2), lax.div(me, 2)
    copies = start_half(a_ref, core, held, a_sems)
    share = targets.shape[1]
    spot = pl.multiple_of(core * held.shape[1] + chip * share, LANES)
    labels_copy = pltpu.make_async_copy(labels_ref.at[:, pl.ds(spot, share)], targets, labels_sem)
    labels_copy.start()
    multiply_half(stacked[...], copies, held, mine)
    labels_copy.wait()


def weighted_kernel(arrived, targets, copies):
    rows = copies.shape[1]
    probes = rows // 2
    margins = jnp.sum(arrived[...].astype(jnp.float32), 0)
    likely = 1.0 / (1.0 + jnp.exp(-margins[:probes]))
    weighted = jnp.concatenate(
        [likely - targets[...].astype(jnp.float32), likely * (1.0 - likely) * margins[probes:]], 0
    ).astype(jnp.bfloat16)
    copies[...] = jnp.broadcast_to(weighted[None], copies.shape)


def fit_kernel(side, weighted, base, a_ref, out, flat, held, sems):
    core = lax.rem(lax.axis_index("feat"), 2)
    copies = start_half(a_ref, core if side == 0 else 1 - core, held, sems)
    for k in range(weighted.shape[0]):
        flat[:, k * LANES : (k + 1) * LANES] = weighted[k]
    total = base[...]
    piece = held.shape[1] // PIECES
    for i, copy in enumerate(copies):
        copy.wait()
        at = slice(i * piece, (i + 1) * piece)
        total = total + transposed_dot(flat[:, at], held[:, at])
    out[...] = total


def local(activations, labels, probe_weights, direction, group_ids):
    probes, width = probe_weights.shape
    rows = 2 * probes
    tokens = activations.shape[0]
    half = tokens // 2
    planes = lax.axis_size("tok")
    devices = lax.axis_size("feat")
    chips = devices // 2
    share = half // chips
    by_core = [[2 * i + side for i in range(chips)] for side in range(2)]
    swap = [(i, i ^ 1) for i in range(devices)]
    along = [(2 * i, 2 * i + 2) for i in range(chips - 1)]
    along += [(2 * i + 3, 2 * i + 1) for i in range(chips - 1)]
    f32, bf16 = jnp.float32, jnp.bfloat16
    vmem, hbm = pl.BlockSpec(memory_space=pltpu.VMEM), pl.BlockSpec(memory_space=pltpu.HBM)
    held = [pltpu.VMEM((width, half), bf16)]
    limit = pltpu.CompilerParams(vmem_limit_bytes=16 << 20)
    half_cost = pl.CostEstimate(
        flops=2 * rows * width * half, bytes_accessed=2 * width * half, transcendentals=0
    )

    def stay(value):
        return pltpu.with_memory_space_constraint(value, pltpu.HBM)

    by_neuron = stay(activations.T)
    theirs, stacked, ids = pl.pallas_call(
        margins_theirs_kernel,
        out_shape=[
            jax.ShapeDtypeStruct((chips + 1, rows, share), f32),
            jax.ShapeDtypeStruct((rows, width), bf16),
            jax.ShapeDtypeStruct((1, width), jnp.int32),
        ],
        in_specs=[hbm] * 4,
        out_specs=[vmem] * 3,
        scratch_shapes=[
            pltpu.VMEM((probes, width), bf16),
            pltpu.VMEM((probes, width), bf16),
            *held,
            pltpu.SemaphoreType.DMA((3,)),
            pltpu.SemaphoreType.DMA((PIECES,)),
        ],
        compiler_params=limit,
        cost_estimate=half_cost,
        name="margins_theirs",
    )(stay(probe_weights), stay(direction), stay(group_ids[None, :]), by_neuron)
    from_pair = lax.ppermute(theirs, "feat", swap)
    mine, targets = pl.pallas_call(
        margins_mine_kernel,
        out_shape=[
            jax.ShapeDtypeStruct((chips, rows, share), f32),
            jax.ShapeDtypeStruct((probes, share), jnp.int32),
        ],
        in_specs=[vmem, hbm, hbm],
        out_specs=[vmem] * 2,
        scratch_shapes=[*held, pltpu.SemaphoreType.DMA, pltpu.SemaphoreType.DMA((PIECES,))],
        compiler_params=limit,
        cost_estimate=half_cost,
        name="margins_mine",
    )(stacked, stay(labels), by_neuron)

    stats = theirs[chips, :, :GROUPS] + from_pair[chips, :, :GROUPS]
    outgoing = (mine + from_pair[:chips]).astype(bf16)
    beside = lax.ppermute(stats, "feat", along)
    arrived = lax.all_to_all(outgoing, "feat", 0, 0, axis_index_groups=by_core)
    copies = pl.pallas_call(
        weighted_kernel,
        out_shape=jax.ShapeDtypeStruct((chips, rows, share), bf16),
        in_specs=[vmem] * 2,
        out_specs=vmem,
        compiler_params=pltpu.CompilerParams(vmem_limit_bytes=4 << 20),
        name="weighted",
    )(arrived, targets)
    weighted_mine = lax.all_to_all(copies, "feat", 0, 0, axis_index_groups=by_core)
    weighted_theirs = lax.ppermute(weighted_mine, "feat", swap)

    def fit(side, weighted, base):
        def kernel(*refs):
            fit_kernel(side, *refs)

        return pl.pallas_call(
            kernel,
            out_shape=jax.ShapeDtypeStruct((rows, width), f32),
            in_specs=[vmem, vmem, hbm],
            out_specs=vmem,
            scratch_shapes=[
                pltpu.VMEM((rows, half), bf16),
                *held,
                pltpu.SemaphoreType.DMA((PIECES,)),
            ],
            compiler_params=limit,
            cost_estimate=half_cost,
            name=("fit_mine", "fit_theirs")[side],
        )(weighted, base, by_neuron)

    fit_mine = fit(0, weighted_mine, jnp.zeros((rows, width), f32))
    local_fit = fit(1, weighted_theirs, fit_mine)
    one, two, three = (
        lax.ppermute(local_fit, "tok", [(i, (i + hop) % planes) for i in range(planes)])
        for hop in (1, 2, 3)
    )
    fitted = (local_fit + two) + (one + three)
    fitted = fitted / math.sqrt(tokens * planes)

    weighted_theirs, beside = lax.optimization_barrier((weighted_theirs, beside))
    totals = stats + (beside + lax.ppermute(beside, "feat", swap))
    wide_weights = stacked[:probes].astype(f32)
    wide_direction = stacked[probes:].astype(f32)
    member = (ids == jnp.arange(GROUPS, dtype=jnp.int32)[:, None]).astype(f32)
    group_norm = jnp.sqrt(totals[:probes] + DELTA * DELTA)
    spread = jnp.dot(
        jnp.concatenate([group_norm, totals[probes:]], 0),
        member,
        precision=lax.Precision.HIGHEST,
        preferred_element_type=f32,
    )
    scale = spread[:probes]
    cross = spread[probes:]
    gradient = fitted[:probes] + LAMBDA_WEIGHT * wide_weights / scale
    hess_vec = fitted[probes:] + LAMBDA_WEIGHT * (
        wide_direction / scale - wide_weights * cross / (scale * scale * scale)
    )
    return (gradient, hess_vec)


def solution(mesh):
    return jax.shard_map(
        local,
        mesh=mesh,
        in_specs=(P("tok", "feat"), P(None, "tok"), P(None, "feat"), P(None, "feat"), P("feat")),
        out_specs=(P(None, "feat"), P(None, "feat")),
        check_vma=False,
    )
```

```python
import math

import jax
import jax.numpy as jnp
from jax import lax
from jax.experimental import pallas as pl
from jax.experimental.pallas import tpu as pltpu
from jax.sharding import PartitionSpec as P

GROUPS = 64


DELTA = 0.05
LAMBDA_WEIGHT = 8.0

LANES = 128
PIECES = 4


def transposed_dot(left, right, precision=None):
    return lax.dot_general(
        left,
        right,
        (((1,), (1,)), ((), ())),
        precision=precision,
        preferred_element_type=jnp.float32,
    )


def start_half(a_ref, side, held, sems):
    half = held.shape[1]
    piece = half // PIECES
    copies = []
    for i in range(PIECES):
        start = pl.multiple_of(side * half + i * piece, LANES)
        copy = pltpu.make_async_copy(
            a_ref.at[:, pl.ds(start, piece)], held.at[:, pl.ds(i * piece, piece)], sems.at[i]
        )
        copy.start()
        copies.append(copy)
    return copies


def multiply_half(stacked, copies, held, out, meanwhile=None):
    piece = held.shape[1] // PIECES
    per_piece = piece // LANES
    for i, copy in enumerate(copies):
        if i == 1 and meanwhile is not None:
            meanwhile()
        copy.wait()
        product = jnp.dot(
            stacked, held[:, i * piece : (i + 1) * piece], preferred_element_type=jnp.float32
        )
        for k in range(per_piece):
            out[i * per_piece + k] = product[:, k * LANES : (k + 1) * LANES]


def margins_theirs_kernel(
    w_ref, d_ref, g_ref, a_ref, theirs, stacked_out, ids_out, w, d, held, small_sems, a_sems
):
    core = lax.rem(lax.axis_index("feat"), 2)
    small = [
        pltpu.make_async_copy(source, target, small_sems.at[i])
        for i, (source, target) in enumerate(((w_ref, w), (d_ref, d), (g_ref, ids_out)))
    ]
    for copy in small:
        copy.start()
    copies = start_half(a_ref, 1 - core, held, a_sems)
    for copy in small:
        copy.wait()
    stacked = jnp.concatenate([w[...], d[...]], 0)
    stacked_out[...] = stacked

    def sum_groups():
        wide_weights = w[...].astype(jnp.float32)
        products = jnp.concatenate(
            [wide_weights * wide_weights, wide_weights * d[...].astype(jnp.float32)], 0
        )
        high = products.astype(jnp.bfloat16)
        low = (products - high.astype(jnp.float32)).astype(jnp.bfloat16)
        number = lax.broadcasted_iota(jnp.int32, (LANES, ids_out.shape[1]), 0)
        member = (number == ids_out[...]).astype(jnp.float32).astype(jnp.bfloat16)
        sums = transposed_dot(jnp.concatenate([high, low], 0), member)
        rows = stacked.shape[0]
        theirs[theirs.shape[0] - 1] = sums[:rows] + sums[rows:]

    multiply_half(stacked, copies, held, theirs, sum_groups)


def margins_mine_kernel(stacked, labels_ref, a_ref, mine, targets, held, labels_sem, a_sems):
    me = lax.axis_index("feat")
    core, chip = lax.rem(me, 2), lax.div(me, 2)
    copies = start_half(a_ref, core, held, a_sems)
    share = targets.shape[1]
    spot = pl.multiple_of(core * held.shape[1] + chip * share, LANES)
    labels_copy = pltpu.make_async_copy(labels_ref.at[:, pl.ds(spot, share)], targets, labels_sem)
    labels_copy.start()
    multiply_half(stacked[...], copies, held, mine)
    labels_copy.wait()


def weighted_kernel(arrived, targets, copies):
    rows = copies.shape[1]
    probes = rows // 2
    margins = jnp.sum(arrived[...].astype(jnp.float32), 0)
    likely = 1.0 / (1.0 + jnp.exp(-margins[:probes]))
    weighted = jnp.concatenate(
        [likely - targets[...].astype(jnp.float32), likely * (1.0 - likely) * margins[probes:]], 0
    ).astype(jnp.bfloat16)
    copies[...] = jnp.broadcast_to(weighted[None], copies.shape)


def flatten(weighted, flat):
    for k in range(weighted.shape[0]):
        flat[:, k * LANES : (k + 1) * LANES] = weighted[k]


def fit_mine_kernel(weighted, a_ref, out, theirs, flat, mine, mine_sems, theirs_sems):
    core = lax.rem(lax.axis_index("feat"), 2)
    copies = start_half(a_ref, core, mine, mine_sems)
    others = start_half(a_ref, 1 - core, theirs, theirs_sems)
    flatten(weighted, flat)
    total = jnp.zeros(out.shape, jnp.float32)
    piece = mine.shape[1] // PIECES
    for i, copy in enumerate(copies):
        copy.wait()
        at = slice(i * piece, (i + 1) * piece)
        total = total + transposed_dot(flat[:, at], mine[:, at])
    out[...] = total
    for copy in others:
        copy.wait()


def fit_theirs_kernel(weighted, theirs, base, out, flat):
    flatten(weighted, flat)
    out[...] = base[...] + transposed_dot(flat[...], theirs[...])


def local(activations, labels, probe_weights, direction, group_ids):
    probes, width = probe_weights.shape
    rows = 2 * probes
    tokens = activations.shape[0]
    half = tokens // 2
    planes = lax.axis_size("tok")
    devices = lax.axis_size("feat")
    chips = devices // 2
    share = half // chips
    by_core = [[2 * i + side for i in range(chips)] for side in range(2)]
    swap = [(i, i ^ 1) for i in range(devices)]
    along = [(2 * i, 2 * i + 2) for i in range(chips - 1)]
    along += [(2 * i + 3, 2 * i + 1) for i in range(chips - 1)]
    f32, bf16 = jnp.float32, jnp.bfloat16
    vmem, hbm = pl.BlockSpec(memory_space=pltpu.VMEM), pl.BlockSpec(memory_space=pltpu.HBM)
    held = [pltpu.VMEM((width, half), bf16)]
    limit = pltpu.CompilerParams(vmem_limit_bytes=16 << 20)
    half_cost = pl.CostEstimate(
        flops=2 * rows * width * half, bytes_accessed=2 * width * half, transcendentals=0
    )

    def stay(value):
        return pltpu.with_memory_space_constraint(value, pltpu.HBM)

    by_neuron = stay(activations.T)
    theirs, stacked, ids = pl.pallas_call(
        margins_theirs_kernel,
        out_shape=[
            jax.ShapeDtypeStruct((chips + 1, rows, share), f32),
            jax.ShapeDtypeStruct((rows, width), bf16),
            jax.ShapeDtypeStruct((1, width), jnp.int32),
        ],
        in_specs=[hbm] * 4,
        out_specs=[vmem] * 3,
        scratch_shapes=[
            pltpu.VMEM((probes, width), bf16),
            pltpu.VMEM((probes, width), bf16),
            *held,
            pltpu.SemaphoreType.DMA((3,)),
            pltpu.SemaphoreType.DMA((PIECES,)),
        ],
        compiler_params=limit,
        cost_estimate=half_cost,
        name="margins_theirs",
    )(stay(probe_weights), stay(direction), stay(group_ids[None, :]), by_neuron)
    from_pair = lax.ppermute(theirs, "feat", swap)
    mine, targets = pl.pallas_call(
        margins_mine_kernel,
        out_shape=[
            jax.ShapeDtypeStruct((chips, rows, share), f32),
            jax.ShapeDtypeStruct((probes, share), jnp.int32),
        ],
        in_specs=[vmem, hbm, hbm],
        out_specs=[vmem] * 2,
        scratch_shapes=[*held, pltpu.SemaphoreType.DMA, pltpu.SemaphoreType.DMA((PIECES,))],
        compiler_params=limit,
        cost_estimate=half_cost,
        name="margins_mine",
    )(stacked, stay(labels), by_neuron)

    stats = theirs[chips, :, :GROUPS] + from_pair[chips, :, :GROUPS]
    outgoing = (mine + from_pair[:chips]).astype(bf16)
    beside = lax.ppermute(stats, "feat", along)
    arrived = lax.all_to_all(outgoing, "feat", 0, 0, axis_index_groups=by_core)
    arrived, beside = lax.optimization_barrier((arrived, beside))
    copies = pl.pallas_call(
        weighted_kernel,
        out_shape=jax.ShapeDtypeStruct((chips, rows, share), bf16),
        in_specs=[vmem] * 2,
        out_specs=vmem,
        compiler_params=pltpu.CompilerParams(vmem_limit_bytes=4 << 20),
        name="weighted",
    )(arrived, targets)
    weighted_mine = lax.all_to_all(copies, "feat", 0, 0, axis_index_groups=by_core)
    weighted_theirs = lax.ppermute(weighted_mine, "feat", swap)

    flat = pltpu.VMEM((rows, half), bf16)
    fit_mine, a_theirs = pl.pallas_call(
        fit_mine_kernel,
        out_shape=[jax.ShapeDtypeStruct((rows, width), f32), *held],
        in_specs=[vmem, hbm],
        out_specs=[vmem] * 2,
        scratch_shapes=[
            flat,
            *held,
            pltpu.SemaphoreType.DMA((PIECES,)),
            pltpu.SemaphoreType.DMA((PIECES,)),
        ],
        compiler_params=limit,
        cost_estimate=half_cost,
        name="fit_mine",
    )(weighted_mine, by_neuron)
    local_fit = pl.pallas_call(
        fit_theirs_kernel,
        out_shape=jax.ShapeDtypeStruct((rows, width), f32),
        in_specs=[vmem] * 3,
        out_specs=vmem,
        scratch_shapes=[flat],
        compiler_params=limit,
        cost_estimate=half_cost,
        name="fit_theirs",
    )(weighted_theirs, pltpu.with_memory_space_constraint(a_theirs, pltpu.VMEM), fit_mine)
    one, two, three = (
        lax.ppermute(local_fit, "tok", [(i, (i + hop) % planes) for i in range(planes)])
        for hop in (1, 2, 3)
    )
    fitted = (local_fit + two) + (one + three)
    fitted = fitted / math.sqrt(tokens * planes)

    totals = stats + (beside + lax.ppermute(beside, "feat", swap))
    wide_weights = stacked[:probes].astype(f32)
    wide_direction = stacked[probes:].astype(f32)
    member = (ids == jnp.arange(GROUPS, dtype=jnp.int32)[:, None]).astype(f32)
    group_norm = jnp.sqrt(totals[:probes] + DELTA * DELTA)
    spread = jnp.dot(
        jnp.concatenate([group_norm, totals[probes:]], 0),
        member,
        precision=lax.Precision.HIGHEST,
        preferred_element_type=f32,
    )
    scale = spread[:probes]
    cross = spread[probes:]
    gradient = fitted[:probes] + LAMBDA_WEIGHT * wide_weights / scale
    hess_vec = fitted[probes:] + LAMBDA_WEIGHT * (
        wide_direction / scale - wide_weights * cross / (scale * scale * scale)
    )
    return (gradient, hess_vec)


def solution(mesh):
    return jax.shard_map(
        local,
        mesh=mesh,
        in_specs=(P("tok", "feat"), P(None, "tok"), P(None, "feat"), P(None, "feat"), P("feat")),
        out_specs=(P(None, "feat"), P(None, "feat")),
        check_vma=False,
    )
```

```python
import math

import jax
import jax.numpy as jnp
from jax import lax
from jax.experimental import pallas as pl
from jax.experimental.pallas import tpu as pltpu
from jax.sharding import PartitionSpec as P

GROUPS = 64


DELTA = 0.05
LAMBDA_WEIGHT = 8.0

LANES = 128
PIECES = 4


def transposed_dot(left, right, precision=None):
    return lax.dot_general(
        left,
        right,
        (((1,), (1,)), ((), ())),
        precision=precision,
        preferred_element_type=jnp.float32,
    )


def start_half(a_ref, side, held, sems):
    half = held.shape[1]
    piece = half // PIECES
    copies = []
    for i in range(PIECES):
        start = pl.multiple_of(side * half + i * piece, LANES)
        copy = pltpu.make_async_copy(
            a_ref.at[:, pl.ds(start, piece)], held.at[:, pl.ds(i * piece, piece)], sems.at[i]
        )
        copy.start()
        copies.append(copy)
    return copies


def multiply_half(stacked, copies, held, out, meanwhile=None):
    piece = held.shape[1] // PIECES
    per_piece = piece // LANES
    for i, copy in enumerate(copies):
        if i == 1 and meanwhile is not None:
            meanwhile()
        copy.wait()
        product = jnp.dot(
            stacked, held[:, i * piece : (i + 1) * piece], preferred_element_type=jnp.float32
        )
        for k in range(per_piece):
            out[i * per_piece + k] = product[:, k * LANES : (k + 1) * LANES]


def margins_kernel(
    w_ref, d_ref, g_ref, labels_ref, a_ref,
    theirs, mine, stacked_out, ids_out, targets,
    w, d, their_half, my_half, small_sems, their_sems, my_sems,
):
    me = lax.axis_index("feat")
    core, chip = lax.rem(me, 2), lax.div(me, 2)
    share = targets.shape[1]
    spot = pl.multiple_of(core * my_half.shape[1] + chip * share, LANES)
    small = [
        pltpu.make_async_copy(source, target, small_sems.at[i])
        for i, (source, target) in enumerate(
            (
                (w_ref, w),
                (d_ref, d),
                (g_ref, ids_out),
                (labels_ref.at[:, pl.ds(spot, share)], targets),
            )
        )
    ]
    for copy in small:
        copy.start()
    their_copies = start_half(a_ref, 1 - core, their_half, their_sems)
    my_copies = start_half(a_ref, core, my_half, my_sems)
    for copy in small:
        copy.wait()
    stacked = jnp.concatenate([w[...], d[...]], 0)
    stacked_out[...] = stacked

    def sum_groups():
        wide_weights = w[...].astype(jnp.float32)
        products = jnp.concatenate(
            [wide_weights * wide_weights, wide_weights * d[...].astype(jnp.float32)], 0
        )
        high = products.astype(jnp.bfloat16)
        low = (products - high.astype(jnp.float32)).astype(jnp.bfloat16)
        number = lax.broadcasted_iota(jnp.int32, (LANES, ids_out.shape[1]), 0)
        member = (number == ids_out[...]).astype(jnp.float32).astype(jnp.bfloat16)
        sums = transposed_dot(jnp.concatenate([high, low], 0), member)
        rows = stacked.shape[0]
        theirs[theirs.shape[0] - 1] = sums[:rows] + sums[rows:]

    multiply_half(stacked, their_copies, their_half, theirs, sum_groups)
    multiply_half(stacked, my_copies, my_half, mine)


def weighted_kernel(arrived, targets, copies):
    rows = copies.shape[1]
    probes = rows // 2
    margins = jnp.sum(arrived[...].astype(jnp.float32), 0)
    likely = 1.0 / (1.0 + jnp.exp(-margins[:probes]))
    weighted = jnp.concatenate(
        [likely - targets[...].astype(jnp.float32), likely * (1.0 - likely) * margins[probes:]], 0
    ).astype(jnp.bfloat16)
    copies[...] = jnp.broadcast_to(weighted[None], copies.shape)


def flatten(weighted, flat):
    for k in range(weighted.shape[0]):
        flat[:, k * LANES : (k + 1) * LANES] = weighted[k]


def fit_mine_kernel(weighted, a_ref, out, theirs, flat, mine, mine_sems, theirs_sems):
    core = lax.rem(lax.axis_index("feat"), 2)
    copies = start_half(a_ref, core, mine, mine_sems)
    others = start_half(a_ref, 1 - core, theirs, theirs_sems)
    flatten(weighted, flat)
    total = jnp.zeros(out.shape, jnp.float32)
    piece = mine.shape[1] // PIECES
    for i, copy in enumerate(copies):
        copy.wait()
        at = slice(i * piece, (i + 1) * piece)
        total = total + transposed_dot(flat[:, at], mine[:, at])
    out[...] = total
    for copy in others:
        copy.wait()


def fit_theirs_kernel(weighted, theirs, base, out, flat):
    flatten(weighted, flat)
    out[...] = base[...] + transposed_dot(flat[...], theirs[...])


def local(activations, labels, probe_weights, direction, group_ids):
    probes, width = probe_weights.shape
    rows = 2 * probes
    tokens = activations.shape[0]
    half = tokens // 2
    planes = lax.axis_size("tok")
    devices = lax.axis_size("feat")
    chips = devices // 2
    share = half // chips
    by_core = [[2 * i + side for i in range(chips)] for side in range(2)]
    swap = [(i, i ^ 1) for i in range(devices)]
    along = [(2 * i, 2 * i + 2) for i in range(chips - 1)]
    along += [(2 * i + 3, 2 * i + 1) for i in range(chips - 1)]
    f32, bf16 = jnp.float32, jnp.bfloat16
    vmem, hbm = pl.BlockSpec(memory_space=pltpu.VMEM), pl.BlockSpec(memory_space=pltpu.HBM)

    def stay(value):
        return pltpu.with_memory_space_constraint(value, pltpu.HBM)

    by_neuron = stay(activations.T)
    theirs, mine, stacked, ids, targets = pl.pallas_call(
        margins_kernel,
        out_shape=[
            jax.ShapeDtypeStruct((chips + 1, rows, share), f32),
            jax.ShapeDtypeStruct((chips, rows, share), f32),
            jax.ShapeDtypeStruct((rows, width), bf16),
            jax.ShapeDtypeStruct((1, width), jnp.int32),
            jax.ShapeDtypeStruct((probes, share), jnp.int32),
        ],
        in_specs=[hbm] * 5,
        out_specs=[vmem] * 5,
        scratch_shapes=[
            pltpu.VMEM((probes, width), bf16),
            pltpu.VMEM((probes, width), bf16),
            pltpu.VMEM((width, half), bf16),
            pltpu.VMEM((width, half), bf16),
            pltpu.SemaphoreType.DMA((4,)),
            pltpu.SemaphoreType.DMA((PIECES,)),
            pltpu.SemaphoreType.DMA((PIECES,)),
        ],
        compiler_params=pltpu.CompilerParams(vmem_limit_bytes=16 << 20),
        name="margins",
    )(
        stay(probe_weights),
        stay(direction),
        stay(group_ids[None, :]),
        stay(labels),
        by_neuron,
    )
    from_pair = lax.ppermute(theirs, "feat", swap)
    stats = theirs[chips, :, :GROUPS] + from_pair[chips, :, :GROUPS]
    outgoing = (mine + from_pair[:chips]).astype(bf16)
    beside = lax.ppermute(stats, "feat", along)
    arrived = lax.all_to_all(outgoing, "feat", 0, 0, axis_index_groups=by_core)
    arrived, beside = lax.optimization_barrier((arrived, beside))
    copies = pl.pallas_call(
        weighted_kernel,
        out_shape=jax.ShapeDtypeStruct((chips, rows, share), bf16),
        in_specs=[vmem] * 2,
        out_specs=vmem,
        compiler_params=pltpu.CompilerParams(vmem_limit_bytes=4 << 20),
        name="weighted",
    )(arrived, targets)
    weighted_mine = lax.all_to_all(copies, "feat", 0, 0, axis_index_groups=by_core)
    weighted_theirs = lax.ppermute(weighted_mine, "feat", swap)

    flat, held = pltpu.VMEM((rows, half), bf16), [pltpu.VMEM((width, half), bf16)]
    limit = pltpu.CompilerParams(vmem_limit_bytes=16 << 20)
    half_cost = pl.CostEstimate(
        flops=2 * rows * width * half, bytes_accessed=4 * width * half, transcendentals=0
    )
    fit_mine, a_theirs = pl.pallas_call(
        fit_mine_kernel,
        out_shape=[jax.ShapeDtypeStruct((rows, width), f32), *held],
        in_specs=[vmem, hbm],
        out_specs=[vmem] * 2,
        scratch_shapes=[
            flat,
            *held,
            pltpu.SemaphoreType.DMA((PIECES,)),
            pltpu.SemaphoreType.DMA((PIECES,)),
        ],
        compiler_params=limit,
        cost_estimate=half_cost,
        name="fit_mine",
    )(weighted_mine, by_neuron)
    weighted_theirs, beside = lax.optimization_barrier((weighted_theirs, beside))
    local_fit = pl.pallas_call(
        fit_theirs_kernel,
        out_shape=jax.ShapeDtypeStruct((rows, width), f32),
        in_specs=[vmem] * 3,
        out_specs=vmem,
        scratch_shapes=[flat],
        compiler_params=limit,
        cost_estimate=half_cost,
        name="fit_theirs",
    )(weighted_theirs, pltpu.with_memory_space_constraint(a_theirs, pltpu.VMEM), fit_mine)
    one, two, three = (
        lax.ppermute(local_fit, "tok", [(i, (i + hop) % planes) for i in range(planes)])
        for hop in (1, 2, 3)
    )
    fitted = (local_fit + two) + (one + three)
    fitted = fitted / math.sqrt(tokens * planes)

    totals = stats + (beside + lax.ppermute(beside, "feat", swap))
    wide_weights = stacked[:probes].astype(f32)
    wide_direction = stacked[probes:].astype(f32)
    member = (ids == jnp.arange(GROUPS, dtype=jnp.int32)[:, None]).astype(f32)
    group_norm = jnp.sqrt(totals[:probes] + DELTA * DELTA)
    spread = jnp.dot(
        jnp.concatenate([group_norm, totals[probes:]], 0),
        member,
        precision=lax.Precision.HIGHEST,
        preferred_element_type=f32,
    )
    scale = spread[:probes]
    cross = spread[probes:]
    gradient = fitted[:probes] + LAMBDA_WEIGHT * wide_weights / scale
    hess_vec = fitted[probes:] + LAMBDA_WEIGHT * (
        wide_direction / scale - wide_weights * cross / (scale * scale * scale)
    )
    return (gradient, hess_vec)


def solution(mesh):
    return jax.shard_map(
        local,
        mesh=mesh,
        in_specs=(P("tok", "feat"), P(None, "tok"), P(None, "feat"), P(None, "feat"), P("feat")),
        out_specs=(P(None, "feat"), P(None, "feat")),
        check_vma=False,
    )
```

```python
import math

import jax
import jax.numpy as jnp
from jax import lax
from jax.experimental import pallas as pl
from jax.experimental.pallas import tpu as pltpu
from jax.sharding import PartitionSpec as P

GROUPS = 64


DELTA = 0.05
LAMBDA_WEIGHT = 8.0

LANES = 128
PIECES = 4


def transposed_dot(left, right, precision=None):
    return lax.dot_general(
        left,
        right,
        (((1,), (1,)), ((), ())),
        precision=precision,
        preferred_element_type=jnp.float32,
    )


def start_half(a_ref, side, held, sems):
    half = held.shape[1]
    piece = half // PIECES
    copies = []
    for i in range(PIECES):
        start = pl.multiple_of(side * half + i * piece, LANES)
        copy = pltpu.make_async_copy(
            a_ref.at[:, pl.ds(start, piece)], held.at[:, pl.ds(i * piece, piece)], sems.at[i]
        )
        copy.start(priority=1)
        copies.append(copy)
    return copies


def multiply_half(stacked, copies, held, out, meanwhile=None):
    piece = held.shape[1] // PIECES
    per_piece = piece // LANES
    for i, copy in enumerate(copies):
        if i == 1 and meanwhile is not None:
            meanwhile()
        copy.wait()
        product = jnp.dot(
            stacked, held[:, i * piece : (i + 1) * piece], preferred_element_type=jnp.float32
        )
        for k in range(per_piece):
            out[i * per_piece + k] = product[:, k * LANES : (k + 1) * LANES]


def margins_theirs_kernel(
    w_ref, d_ref, g_ref, a_ref,
    theirs, stats, stacked_out, ids_out,
    w, d, held, small_sems, a_sems,
):
    core = lax.rem(lax.axis_index("feat"), 2)
    small = [
        pltpu.make_async_copy(source, target, small_sems.at[i])
        for i, (source, target) in enumerate(((w_ref, w), (d_ref, d), (g_ref, ids_out)))
    ]
    for copy in small:
        copy.start()
    copies = start_half(a_ref, 1 - core, held, a_sems)
    for copy in small:
        copy.wait()
    stacked = jnp.concatenate([w[...], d[...]], 0)
    stacked_out[...] = stacked

    def sum_groups():
        wide_weights = w[...].astype(jnp.float32)
        products = jnp.concatenate(
            [wide_weights * wide_weights, wide_weights * d[...].astype(jnp.float32)], 0
        )
        high = products.astype(jnp.bfloat16)
        low = (products - high.astype(jnp.float32)).astype(jnp.bfloat16)
        number = lax.broadcasted_iota(jnp.int32, (LANES, ids_out.shape[1]), 0)
        member = (number == ids_out[...]).astype(jnp.float32).astype(jnp.bfloat16)
        sums = transposed_dot(jnp.concatenate([high, low], 0), member)
        rows = stacked.shape[0]
        stats[...] = sums[:rows] + sums[rows:]

    multiply_half(stacked, copies, held, theirs, sum_groups)


def margins_mine_kernel(stacked, labels_ref, a_ref, mine, targets, held, labels_sem, a_sems):
    me = lax.axis_index("feat")
    core, chip = lax.rem(me, 2), lax.div(me, 2)
    copies = start_half(a_ref, core, held, a_sems)
    share = targets.shape[1]
    spot = pl.multiple_of(core * held.shape[1] + chip * share, LANES)
    labels_copy = pltpu.make_async_copy(labels_ref.at[:, pl.ds(spot, share)], targets, labels_sem)
    labels_copy.start()
    multiply_half(stacked[...], copies, held, mine)
    labels_copy.wait()


def weighted_kernel(arrived, targets, copies):
    rows = copies.shape[1]
    probes = rows // 2
    margins = jnp.sum(arrived[...].astype(jnp.float32), 0)
    likely = 1.0 / (1.0 + jnp.exp(-margins[:probes]))
    weighted = jnp.concatenate(
        [likely - targets[...].astype(jnp.float32), likely * (1.0 - likely) * margins[probes:]], 0
    ).astype(jnp.bfloat16)
    copies[...] = jnp.broadcast_to(weighted[None], copies.shape)


def flatten(weighted, flat):
    for k in range(weighted.shape[0]):
        flat[:, k * LANES : (k + 1) * LANES] = weighted[k]


def fit_mine_kernel(weighted, a_ref, out, theirs, flat, mine, mine_sems, theirs_sems):
    core = lax.rem(lax.axis_index("feat"), 2)
    copies = start_half(a_ref, core, mine, mine_sems)
    others = start_half(a_ref, 1 - core, theirs, theirs_sems)
    flatten(weighted, flat)
    total = jnp.zeros(out.shape, jnp.float32)
    piece = mine.shape[1] // PIECES
    for i, copy in enumerate(copies):
        copy.wait()
        at = slice(i * piece, (i + 1) * piece)
        total = total + transposed_dot(flat[:, at], mine[:, at])
    out[...] = total
    for copy in others:
        copy.wait()


def fit_theirs_kernel(weighted, theirs, base, out, flat):
    flatten(weighted, flat)
    out[...] = base[...] + transposed_dot(flat[...], theirs[...])


def local(activations, labels, probe_weights, direction, group_ids):
    probes, width = probe_weights.shape
    rows = 2 * probes
    tokens = activations.shape[0]
    half = tokens // 2
    planes = lax.axis_size("tok")
    devices = lax.axis_size("feat")
    chips = devices // 2
    share = half // chips
    by_core = [[2 * i + side for i in range(chips)] for side in range(2)]
    swap = [(i, i ^ 1) for i in range(devices)]
    along = [(2 * i, 2 * i + 2) for i in range(chips - 1)]
    along += [(2 * i + 3, 2 * i + 1) for i in range(chips - 1)]
    f32, bf16 = jnp.float32, jnp.bfloat16
    vmem, hbm = pl.BlockSpec(memory_space=pltpu.VMEM), pl.BlockSpec(memory_space=pltpu.HBM)
    held = [pltpu.VMEM((width, half), bf16)]
    limit = pltpu.CompilerParams(vmem_limit_bytes=16 << 20)
    half_cost = pl.CostEstimate(
        flops=2 * rows * width * half, bytes_accessed=2 * width * half, transcendentals=0
    )

    def stay(value):
        return pltpu.with_memory_space_constraint(value, pltpu.HBM)

    by_neuron = stay(activations.T)
    theirs, stats, stacked, ids = pl.pallas_call(
        margins_theirs_kernel,
        out_shape=[
            jax.ShapeDtypeStruct((chips, rows, share), f32),
            jax.ShapeDtypeStruct((rows, LANES), f32),
            jax.ShapeDtypeStruct((rows, width), bf16),
            jax.ShapeDtypeStruct((1, width), jnp.int32),
        ],
        in_specs=[hbm] * 4,
        out_specs=[vmem] * 4,
        scratch_shapes=[
            pltpu.VMEM((probes, width), bf16),
            pltpu.VMEM((probes, width), bf16),
            *held,
            pltpu.SemaphoreType.DMA((3,)),
            pltpu.SemaphoreType.DMA((PIECES,)),
        ],
        compiler_params=limit,
        cost_estimate=half_cost,
        name="margins_theirs",
    )(stay(probe_weights), stay(direction), stay(group_ids[None, :]), by_neuron)
    stats = stats + lax.ppermute(stats, "feat", swap)
    stacked, theirs, stats = lax.optimization_barrier((stacked, theirs, stats))
    beside = lax.ppermute(stats, "feat", along)
    from_pair = lax.ppermute(theirs, "feat", swap)
    mine, targets = pl.pallas_call(
        margins_mine_kernel,
        out_shape=[
            jax.ShapeDtypeStruct((chips, rows, share), f32),
            jax.ShapeDtypeStruct((probes, share), jnp.int32),
        ],
        in_specs=[vmem, hbm, hbm],
        out_specs=[vmem] * 2,
        scratch_shapes=[*held, pltpu.SemaphoreType.DMA, pltpu.SemaphoreType.DMA((PIECES,))],
        compiler_params=limit,
        cost_estimate=half_cost,
        name="margins_mine",
    )(stacked, stay(labels), by_neuron)

    outgoing, beside = lax.optimization_barrier(((mine + from_pair).astype(bf16), beside))
    arrived = lax.all_to_all(outgoing, "feat", 0, 0, axis_index_groups=by_core)
    copies = pl.pallas_call(
        weighted_kernel,
        out_shape=jax.ShapeDtypeStruct((chips, rows, share), bf16),
        in_specs=[vmem] * 2,
        out_specs=vmem,
        compiler_params=pltpu.CompilerParams(vmem_limit_bytes=4 << 20),
        name="weighted",
    )(arrived, targets)
    weighted_mine = lax.all_to_all(copies, "feat", 0, 0, axis_index_groups=by_core)
    weighted_theirs = lax.ppermute(weighted_mine, "feat", swap)

    flat = pltpu.VMEM((rows, half), bf16)
    fit_mine, a_theirs = pl.pallas_call(
        fit_mine_kernel,
        out_shape=[jax.ShapeDtypeStruct((rows, width), f32), *held],
        in_specs=[vmem, hbm],
        out_specs=[vmem] * 2,
        scratch_shapes=[
            flat,
            *held,
            pltpu.SemaphoreType.DMA((PIECES,)),
            pltpu.SemaphoreType.DMA((PIECES,)),
        ],
        compiler_params=limit,
        cost_estimate=half_cost,
        name="fit_mine",
    )(weighted_mine, by_neuron)
    local_fit = pl.pallas_call(
        fit_theirs_kernel,
        out_shape=jax.ShapeDtypeStruct((rows, width), f32),
        in_specs=[vmem] * 3,
        out_specs=vmem,
        scratch_shapes=[flat],
        compiler_params=limit,
        cost_estimate=half_cost,
        name="fit_theirs",
    )(weighted_theirs, pltpu.with_memory_space_constraint(a_theirs, pltpu.VMEM), fit_mine)
    local_fit, beside = lax.optimization_barrier((local_fit, beside))
    one, two, three = (
        lax.ppermute(local_fit, "tok", [(i, (i + hop) % planes) for i in range(planes)])
        for hop in (1, 2, 3)
    )
    fitted = (local_fit + two) + (one + three)
    fitted = fitted / math.sqrt(tokens * planes)

    totals = (stats + (beside + lax.ppermute(beside, "feat", swap)))[:, :GROUPS]
    wide_weights = stacked[:probes].astype(f32)
    wide_direction = stacked[probes:].astype(f32)
    member = (ids == jnp.arange(GROUPS, dtype=jnp.int32)[:, None]).astype(f32)
    group_norm = jnp.sqrt(totals[:probes] + DELTA * DELTA)
    spread = jnp.dot(
        jnp.concatenate([group_norm, totals[probes:]], 0),
        member,
        precision=lax.Precision.HIGHEST,
        preferred_element_type=f32,
    )
    scale = spread[:probes]
    cross = spread[probes:]
    gradient = fitted[:probes] + LAMBDA_WEIGHT * wide_weights / scale
    hess_vec = fitted[probes:] + LAMBDA_WEIGHT * (
        wide_direction / scale - wide_weights * cross / (scale * scale * scale)
    )
    return (gradient, hess_vec)


def solution(mesh):
    return jax.shard_map(
        local,
        mesh=mesh,
        in_specs=(P("tok", "feat"), P(None, "tok"), P(None, "feat"), P(None, "feat"), P("feat")),
        out_specs=(P(None, "feat"), P(None, "feat")),
        check_vma=False,
    )
```

```python
import math

import jax
import jax.numpy as jnp
from jax import lax
from jax.experimental import pallas as pl
from jax.experimental.pallas import tpu as pltpu
from jax.sharding import PartitionSpec as P

GROUPS = 64


DELTA = 0.05
LAMBDA_WEIGHT = 8.0

LANES = 128
PIECES = 4


def transposed_dot(left, right, precision=None):
    return lax.dot_general(
        left,
        right,
        (((1,), (1,)), ((), ())),
        precision=precision,
        preferred_element_type=jnp.float32,
    )


def start_half(a_ref, side, held, sems):
    half = held.shape[1]
    piece = half // PIECES
    copies = []
    for i in range(PIECES):
        start = pl.multiple_of(side * half + i * piece, LANES)
        copy = pltpu.make_async_copy(
            a_ref.at[:, pl.ds(start, piece)], held.at[:, pl.ds(i * piece, piece)], sems.at[i]
        )
        copy.start(priority=1)
        copies.append(copy)
    return copies


def multiply_half(stacked, copies, held, out, meanwhile=None):
    piece = held.shape[1] // PIECES
    per_piece = piece // LANES
    for i, copy in enumerate(copies):
        if i == 1 and meanwhile is not None:
            meanwhile()
        copy.wait()
        product = jnp.dot(
            stacked, held[:, i * piece : (i + 1) * piece], preferred_element_type=jnp.float32
        )
        for k in range(per_piece):
            out[i * per_piece + k] = product[:, k * LANES : (k + 1) * LANES]


def margins_theirs_kernel(
    w_ref, d_ref, g_ref, a_ref, theirs, stacked_out, ids_out, w, d, held, small_sems, a_sems
):
    core = lax.rem(lax.axis_index("feat"), 2)
    small = [
        pltpu.make_async_copy(source, target, small_sems.at[i])
        for i, (source, target) in enumerate(((w_ref, w), (d_ref, d), (g_ref, ids_out)))
    ]
    for copy in small:
        copy.start()
    copies = start_half(a_ref, 1 - core, held, a_sems)
    for copy in small:
        copy.wait()
    stacked = jnp.concatenate([w[...], d[...]], 0)
    stacked_out[...] = stacked

    def sum_groups():
        wide_weights = w[...].astype(jnp.float32)
        products = jnp.concatenate(
            [wide_weights * wide_weights, wide_weights * d[...].astype(jnp.float32)], 0
        )
        high = products.astype(jnp.bfloat16)
        low = (products - high.astype(jnp.float32)).astype(jnp.bfloat16)
        number = lax.broadcasted_iota(jnp.int32, (LANES, ids_out.shape[1]), 0)
        member = (number == ids_out[...]).astype(jnp.float32).astype(jnp.bfloat16)
        sums = transposed_dot(jnp.concatenate([high, low], 0), member)
        rows = stacked.shape[0]
        theirs[theirs.shape[0] - 1] = sums[:rows] + sums[rows:]

    multiply_half(stacked, copies, held, theirs, sum_groups)


def margins_mine_kernel(stacked, labels_ref, a_ref, mine, targets, held, labels_sem, a_sems):
    me = lax.axis_index("feat")
    core, chip = lax.rem(me, 2), lax.div(me, 2)
    copies = start_half(a_ref, core, held, a_sems)
    share = targets.shape[1]
    spot = pl.multiple_of(core * held.shape[1] + chip * share, LANES)
    labels_copy = pltpu.make_async_copy(labels_ref.at[:, pl.ds(spot, share)], targets, labels_sem)
    labels_copy.start()
    multiply_half(stacked[...], copies, held, mine)
    labels_copy.wait()


def weighted_kernel(arrived, targets, copies):
    rows = copies.shape[1]
    probes = rows // 2
    margins = jnp.sum(arrived[...].astype(jnp.float32), 0)
    likely = 1.0 / (1.0 + jnp.exp(-margins[:probes]))
    weighted = jnp.concatenate(
        [likely - targets[...].astype(jnp.float32), likely * (1.0 - likely) * margins[probes:]], 0
    ).astype(jnp.bfloat16)
    copies[...] = jnp.broadcast_to(weighted[None], copies.shape)


def flatten(weighted, flat):
    for k in range(weighted.shape[0]):
        flat[:, k * LANES : (k + 1) * LANES] = weighted[k]


def fit_mine_kernel(weighted, a_ref, out, theirs, flat, mine, mine_sems, theirs_sems):
    core = lax.rem(lax.axis_index("feat"), 2)
    copies = start_half(a_ref, core, mine, mine_sems)
    others = start_half(a_ref, 1 - core, theirs, theirs_sems)
    flatten(weighted, flat)
    total = jnp.zeros(out.shape, jnp.float32)
    piece = mine.shape[1] // PIECES
    for i, copy in enumerate(copies):
        copy.wait()
        at = slice(i * piece, (i + 1) * piece)
        total = total + transposed_dot(flat[:, at], mine[:, at])
    out[...] = total
    for copy in others:
        copy.wait()


def fit_theirs_kernel(weighted, theirs, base, out, flat):
    flatten(weighted, flat)
    out[...] = base[...] + transposed_dot(flat[...], theirs[...])


def local(activations, labels, probe_weights, direction, group_ids):
    probes, width = probe_weights.shape
    rows = 2 * probes
    tokens = activations.shape[0]
    half = tokens // 2
    planes = lax.axis_size("tok")
    devices = lax.axis_size("feat")
    chips = devices // 2
    share = half // chips
    by_core = [[2 * i + side for i in range(chips)] for side in range(2)]
    swap = [(i, i ^ 1) for i in range(devices)]
    along = [(2 * i, (2 * i + 2) % devices) for i in range(chips)]
    along += [((2 * i + 3) % devices, 2 * i + 1) for i in range(chips)]
    f32, bf16 = jnp.float32, jnp.bfloat16
    vmem, hbm = pl.BlockSpec(memory_space=pltpu.VMEM), pl.BlockSpec(memory_space=pltpu.HBM)
    held = [pltpu.VMEM((width, half), bf16)]
    limit = pltpu.CompilerParams(vmem_limit_bytes=16 << 20)
    half_cost = pl.CostEstimate(
        flops=2 * rows * width * half, bytes_accessed=2 * width * half, transcendentals=0
    )

    def stay(value):
        return pltpu.with_memory_space_constraint(value, pltpu.HBM)

    by_neuron = stay(activations.T)
    theirs, stacked, ids = pl.pallas_call(
        margins_theirs_kernel,
        out_shape=[
            jax.ShapeDtypeStruct((chips + 1, rows, share), f32),
            jax.ShapeDtypeStruct((rows, width), bf16),
            jax.ShapeDtypeStruct((1, width), jnp.int32),
        ],
        in_specs=[hbm] * 4,
        out_specs=[vmem] * 3,
        scratch_shapes=[
            pltpu.VMEM((probes, width), bf16),
            pltpu.VMEM((probes, width), bf16),
            *held,
            pltpu.SemaphoreType.DMA((3,)),
            pltpu.SemaphoreType.DMA((PIECES,)),
        ],
        compiler_params=limit,
        cost_estimate=half_cost,
        name="margins_theirs",
    )(stay(probe_weights), stay(direction), stay(group_ids[None, :]), by_neuron)
    from_pair = lax.ppermute(theirs, "feat", swap)
    mine, targets = pl.pallas_call(
        margins_mine_kernel,
        out_shape=[
            jax.ShapeDtypeStruct((chips, rows, share), f32),
            jax.ShapeDtypeStruct((probes, share), jnp.int32),
        ],
        in_specs=[vmem, hbm, hbm],
        out_specs=[vmem] * 2,
        scratch_shapes=[*held, pltpu.SemaphoreType.DMA, pltpu.SemaphoreType.DMA((PIECES,))],
        compiler_params=limit,
        cost_estimate=half_cost,
        name="margins_mine",
    )(stacked, stay(labels), by_neuron)

    stats = theirs[chips, :, :GROUPS] + from_pair[chips, :, :GROUPS]
    outgoing = (mine + from_pair[:chips]).astype(bf16)
    beside = lax.ppermute(stats, "feat", along)
    arrived = lax.all_to_all(outgoing, "feat", 0, 0, axis_index_groups=by_core)
    arrived, beside = lax.optimization_barrier((arrived, beside))
    copies = pl.pallas_call(
        weighted_kernel,
        out_shape=jax.ShapeDtypeStruct((chips, rows, share), bf16),
        in_specs=[vmem] * 2,
        out_specs=vmem,
        compiler_params=pltpu.CompilerParams(vmem_limit_bytes=4 << 20),
        name="weighted",
    )(arrived, targets)
    weighted_mine = lax.all_to_all(copies, "feat", 0, 0, axis_index_groups=by_core)
    weighted_theirs = lax.ppermute(weighted_mine, "feat", swap)

    flat = pltpu.VMEM((rows, half), bf16)
    fit_mine, a_theirs = pl.pallas_call(
        fit_mine_kernel,
        out_shape=[jax.ShapeDtypeStruct((rows, width), f32), *held],
        in_specs=[vmem, hbm],
        out_specs=[vmem] * 2,
        scratch_shapes=[
            flat,
            *held,
            pltpu.SemaphoreType.DMA((PIECES,)),
            pltpu.SemaphoreType.DMA((PIECES,)),
        ],
        compiler_params=limit,
        cost_estimate=half_cost,
        name="fit_mine",
    )(weighted_mine, by_neuron)
    local_fit = pl.pallas_call(
        fit_theirs_kernel,
        out_shape=jax.ShapeDtypeStruct((rows, width), f32),
        in_specs=[vmem] * 3,
        out_specs=vmem,
        scratch_shapes=[flat],
        compiler_params=limit,
        cost_estimate=half_cost,
        name="fit_theirs",
    )(weighted_theirs, pltpu.with_memory_space_constraint(a_theirs, pltpu.VMEM), fit_mine)
    local_fit, beside = lax.optimization_barrier((local_fit, beside))
    one, two, three = (
        lax.ppermute(local_fit, "tok", [(i, (i + hop) % planes) for i in range(planes)])
        for hop in (1, 2, 3)
    )
    fitted = (local_fit + two) + (one + three)
    fitted = fitted / math.sqrt(tokens * planes)

    totals = stats + (beside + lax.ppermute(beside, "feat", swap))
    wide_weights = stacked[:probes].astype(f32)
    wide_direction = stacked[probes:].astype(f32)
    member = (ids == jnp.arange(GROUPS, dtype=jnp.int32)[:, None]).astype(f32)
    group_norm = jnp.sqrt(totals[:probes] + DELTA * DELTA)
    spread = jnp.dot(
        jnp.concatenate([group_norm, totals[probes:]], 0),
        member,
        precision=lax.Precision.HIGHEST,
        preferred_element_type=f32,
    )
    scale = spread[:probes]
    cross = spread[probes:]
    gradient = fitted[:probes] + LAMBDA_WEIGHT * wide_weights / scale
    hess_vec = fitted[probes:] + LAMBDA_WEIGHT * (
        wide_direction / scale - wide_weights * cross / (scale * scale * scale)
    )
    return (gradient, hess_vec)


def solution(mesh):
    return jax.shard_map(
        local,
        mesh=mesh,
        in_specs=(P("tok", "feat"), P(None, "tok"), P(None, "feat"), P(None, "feat"), P("feat")),
        out_specs=(P(None, "feat"), P(None, "feat")),
        check_vma=False,
    )
```

```python
import math

import jax
import jax.numpy as jnp
from jax import lax
from jax.experimental import pallas as pl
from jax.experimental.pallas import tpu as pltpu
from jax.sharding import PartitionSpec as P

GROUPS = 64


DELTA = 0.05
LAMBDA_WEIGHT = 8.0

LANES = 128
PIECES = 4


def transposed_dot(left, right, precision=None):
    return lax.dot_general(
        left,
        right,
        (((1,), (1,)), ((), ())),
        precision=precision,
        preferred_element_type=jnp.float32,
    )


def start_half(a_ref, side, held, sems):
    half = held.shape[1]
    piece = half // PIECES
    copies = []
    for i in range(PIECES):
        start = pl.multiple_of(side * half + i * piece, LANES)
        copy = pltpu.make_async_copy(
            a_ref.at[:, pl.ds(start, piece)], held.at[:, pl.ds(i * piece, piece)], sems.at[i]
        )
        copy.start(priority=1)
        copies.append(copy)
    return copies


def multiply_half(stacked, copies, held, out, meanwhile=None):
    piece = held.shape[1] // PIECES
    per_piece = piece // LANES
    for i, copy in enumerate(copies):
        if i == 1 and meanwhile is not None:
            meanwhile()
        copy.wait()
        product = jnp.dot(
            stacked, held[:, i * piece : (i + 1) * piece], preferred_element_type=jnp.float32
        )
        for k in range(per_piece):
            out[i * per_piece + k] = product[:, k * LANES : (k + 1) * LANES]


def margins_kernel(
    w_ref, d_ref, g_ref, labels_ref, a_ref,
    theirs, mine, stats_mine, stacked_out, ids_out, targets, their_half, my_half,
    w, d, small_sems, their_sems, my_sems,
):
    me = lax.axis_index("feat")
    core, chip = lax.rem(me, 2), lax.div(me, 2)
    share = targets.shape[1]
    spot = pl.multiple_of(core * my_half.shape[1] + chip * share, LANES)
    small = [
        pltpu.make_async_copy(source, target, small_sems.at[i])
        for i, (source, target) in enumerate(
            (
                (w_ref, w),
                (d_ref, d),
                (g_ref, ids_out),
                (labels_ref.at[:, pl.ds(spot, share)], targets),
            )
        )
    ]
    for copy in small:
        copy.start()
    their_copies = start_half(a_ref, 1 - core, their_half, their_sems)
    my_copies = start_half(a_ref, core, my_half, my_sems)
    for copy in small:
        copy.wait()
    stacked = jnp.concatenate([w[...], d[...]], 0)
    stacked_out[...] = stacked

    def sum_groups():
        wide_weights = w[...].astype(jnp.float32)
        products = jnp.concatenate(
            [wide_weights * wide_weights, wide_weights * d[...].astype(jnp.float32)], 0
        )
        high = products.astype(jnp.bfloat16)
        low = (products - high.astype(jnp.float32)).astype(jnp.bfloat16)
        number = lax.broadcasted_iota(jnp.int32, (LANES, ids_out.shape[1]), 0)
        member = (number == ids_out[...]).astype(jnp.float32).astype(jnp.bfloat16)
        sums = transposed_dot(jnp.concatenate([high, low], 0), member)
        rows = stacked.shape[0]
        sums = sums[:rows] + sums[rows:]
        squares, crosses = sums[: rows // 2], sums[rows // 2 :]
        stats_mine[...] = jnp.where(core == 0, squares, crosses)
        theirs[theirs.shape[0] - 1] = jnp.concatenate([jnp.where(core == 0, crosses, squares)] * 2, 0)

    multiply_half(stacked, their_copies, their_half, theirs, sum_groups)
    multiply_half(stacked, my_copies, my_half, mine)


def weighted_kernel(arrived, targets, copies, totals):
    rows = copies.shape[1]
    probes = rows // 2
    summed = jnp.sum(arrived[...].astype(jnp.float32), 0)
    margins, split_stats = summed[:rows], summed[rows:]
    totals[...] = split_stats[:, :GROUPS] + split_stats[:, GROUPS:]
    likely = 1.0 / (1.0 + jnp.exp(-margins[:probes]))
    weighted = jnp.concatenate(
        [likely - targets[...].astype(jnp.float32), likely * (1.0 - likely) * margins[probes:]], 0
    ).astype(jnp.bfloat16)
    copies[...] = jnp.broadcast_to(weighted[None], copies.shape)


def penalty_kernel(totals_mine, totals_theirs, stacked, ids, out):
    core = lax.rem(lax.axis_index("feat"), 2)
    squares = jnp.where(core == 0, totals_mine[...], totals_theirs[...])
    crosses = jnp.where(core == 0, totals_theirs[...], totals_mine[...])
    probes = squares.shape[0]
    number = lax.broadcasted_iota(jnp.int32, (GROUPS, ids.shape[1]), 0)
    member = (number == ids[...]).astype(jnp.float32)
    group_norm = jnp.sqrt(squares + DELTA * DELTA)
    spread = jnp.dot(
        jnp.concatenate([group_norm, crosses], 0),
        member,
        precision=lax.Precision.HIGHEST,
        preferred_element_type=jnp.float32,
    )
    scale, cross = spread[:probes], spread[probes:]
    wide = stacked[...].astype(jnp.float32)
    weights, direction = wide[:probes], wide[probes:]
    out[:probes] = LAMBDA_WEIGHT * weights / scale
    out[probes:] = LAMBDA_WEIGHT * (
        direction / scale - weights * cross / (scale * scale * scale)
    )


def flatten(weighted, flat):
    for k in range(weighted.shape[0]):
        flat[:, k * LANES : (k + 1) * LANES] = weighted[k]


def fit_kernel(weighted, activations, base, out, flat):
    flatten(weighted, flat)
    out[...] = base[...] + transposed_dot(flat[...], activations[...])


def local(activations, labels, probe_weights, direction, group_ids):
    probes, width = probe_weights.shape
    rows = 2 * probes
    tokens = activations.shape[0]
    half = tokens // 2
    planes = lax.axis_size("tok")
    devices = lax.axis_size("feat")
    chips = devices // 2
    share = half // chips
    by_core = [[2 * i + side for i in range(chips)] for side in range(2)]
    swap = [(i, i ^ 1) for i in range(devices)]
    f32, bf16 = jnp.float32, jnp.bfloat16
    vmem, hbm = pl.BlockSpec(memory_space=pltpu.VMEM), pl.BlockSpec(memory_space=pltpu.HBM)
    held = pltpu.VMEM((width, half), bf16)
    half_cost = pl.CostEstimate(
        flops=2 * rows * width * half, bytes_accessed=2 * width * half, transcendentals=0
    )

    def stay(value):
        return pltpu.with_memory_space_constraint(value, pltpu.HBM)

    theirs, mine, stats_mine, stacked, ids, targets, a_theirs, a_mine = pl.pallas_call(
        margins_kernel,
        out_shape=[
            jax.ShapeDtypeStruct((chips + 1, rows, share), f32),
            jax.ShapeDtypeStruct((chips, rows, share), f32),
            jax.ShapeDtypeStruct((probes, LANES), f32),
            jax.ShapeDtypeStruct((rows, width), bf16),
            jax.ShapeDtypeStruct((1, width), jnp.int32),
            jax.ShapeDtypeStruct((probes, share), jnp.int32),
            held,
            held,
        ],
        in_specs=[hbm] * 5,
        out_specs=[vmem] * 8,
        scratch_shapes=[
            pltpu.VMEM((probes, width), bf16),
            pltpu.VMEM((probes, width), bf16),
            pltpu.SemaphoreType.DMA((4,)),
            pltpu.SemaphoreType.DMA((PIECES,)),
            pltpu.SemaphoreType.DMA((PIECES,)),
        ],
        compiler_params=pltpu.CompilerParams(vmem_limit_bytes=16 << 20),
        name="margins",
    )(
        stay(probe_weights),
        stay(direction),
        stay(group_ids[None, :]),
        stay(labels),
        stay(activations.T),
    )
    from_pair = lax.ppermute(theirs, "feat", swap)
    stats = (stats_mine + from_pair[chips, :probes])[:, :GROUPS]
    high = lax.reduce_precision(stats, 8, 7)
    split_stats = jnp.concatenate([high, stats - high], 1).astype(bf16)
    pair_sum = (mine + from_pair[:chips]).astype(bf16)
    outgoing = jnp.concatenate(
        [pair_sum, jnp.broadcast_to(split_stats[None], (chips, probes, 2 * GROUPS))], 1
    )
    arrived = lax.all_to_all(outgoing, "feat", 0, 0, axis_index_groups=by_core)
    copies, totals_mine = pl.pallas_call(
        weighted_kernel,
        out_shape=[
            jax.ShapeDtypeStruct((chips, rows, share), bf16),
            jax.ShapeDtypeStruct((probes, GROUPS), f32),
        ],
        in_specs=[vmem] * 2,
        out_specs=[vmem] * 2,
        compiler_params=pltpu.CompilerParams(vmem_limit_bytes=4 << 20),
        name="weighted",
    )(arrived, targets)
    weighted_mine = lax.all_to_all(copies, "feat", 0, 0, axis_index_groups=by_core)
    weighted_theirs = lax.ppermute(weighted_mine, "feat", swap)


    def fit(name, weighted, activations, base):
        return pl.pallas_call(
            fit_kernel,
            out_shape=jax.ShapeDtypeStruct((rows, width), f32),
            in_specs=[vmem] * 3,
            out_specs=vmem,
            scratch_shapes=[pltpu.VMEM((rows, half), bf16)],
            compiler_params=pltpu.CompilerParams(vmem_limit_bytes=8 << 20),
            cost_estimate=half_cost,
            name=name,
        )(weighted, pltpu.with_memory_space_constraint(activations, pltpu.VMEM), base)

    fit_mine = fit("fit_mine", weighted_mine, a_mine, jnp.zeros((rows, width), f32))
    local_fit = fit("fit_theirs", weighted_theirs, a_theirs, fit_mine)
    local_fit, totals_mine = lax.optimization_barrier((local_fit, totals_mine))
    one, two, three = (
        lax.ppermute(local_fit, "tok", [(i, (i + hop) % planes) for i in range(planes)])
        for hop in (1, 2, 3)
    )
    fitted = (one + three) + (local_fit + two)
    fitted = fitted / math.sqrt(tokens * planes)

    totals_theirs = lax.ppermute(totals_mine, "feat", swap)
    penalty = pl.pallas_call(
        penalty_kernel,
        out_shape=jax.ShapeDtypeStruct((rows, width), f32),
        in_specs=[vmem] * 4,
        out_specs=vmem,
        compiler_params=pltpu.CompilerParams(vmem_limit_bytes=4 << 20),
        name="penalty",
    )(totals_mine, totals_theirs, stacked, ids)
    gradient = fitted[:probes] + penalty[:probes]
    hess_vec = fitted[probes:] + penalty[probes:]
    return (gradient, hess_vec)


def solution(mesh):
    return jax.shard_map(
        local,
        mesh=mesh,
        in_specs=(P("tok", "feat"), P(None, "tok"), P(None, "feat"), P(None, "feat"), P("feat")),
        out_specs=(P(None, "feat"), P(None, "feat")),
        check_vma=False,
    )
```

```python
import math

import jax
import jax.numpy as jnp
from jax import lax
from jax.experimental import pallas as pl
from jax.experimental.pallas import tpu as pltpu
from jax.sharding import PartitionSpec as P

GROUPS = 64


DELTA = 0.05
LAMBDA_WEIGHT = 8.0

LANES = 128
PIECES = 4


def transposed_dot(left, right, precision=None):
    return lax.dot_general(
        left,
        right,
        (((1,), (1,)), ((), ())),
        precision=precision,
        preferred_element_type=jnp.float32,
    )


def start_half(a_ref, side, held, sems):
    half = held.shape[1]
    piece = half // PIECES
    copies = []
    for i in range(PIECES):
        start = pl.multiple_of(side * half + i * piece, LANES)
        copy = pltpu.make_async_copy(
            a_ref.at[:, pl.ds(start, piece)], held.at[:, pl.ds(i * piece, piece)], sems.at[i]
        )
        copy.start(priority=1)
        copies.append(copy)
    return copies


def multiply_half(stacked, copies, held, out, meanwhile=None):
    piece = held.shape[1] // PIECES
    per_piece = piece // LANES
    for i, copy in enumerate(copies):
        if i == 1 and meanwhile is not None:
            meanwhile()
        copy.wait()
        product = jnp.dot(
            stacked, held[:, i * piece : (i + 1) * piece], preferred_element_type=jnp.float32
        )
        for k in range(per_piece):
            out[i * per_piece + k] = product[:, k * LANES : (k + 1) * LANES]


def margins_theirs_kernel(
    w_ref, d_ref, g_ref, a_ref,
    theirs, stats_mine, stacked_out, ids_out, held,
    w, d, small_sems, a_sems,
):
    core = lax.rem(lax.axis_index("feat"), 2)
    small = [
        pltpu.make_async_copy(source, target, small_sems.at[i])
        for i, (source, target) in enumerate(((w_ref, w), (d_ref, d), (g_ref, ids_out)))
    ]
    for copy in small:
        copy.start()
    copies = start_half(a_ref, 1 - core, held, a_sems)
    for copy in small:
        copy.wait()
    stacked = jnp.concatenate([w[...], d[...]], 0)
    stacked_out[...] = stacked

    def sum_groups():
        wide_weights = w[...].astype(jnp.float32)
        products = jnp.concatenate(
            [wide_weights * wide_weights, wide_weights * d[...].astype(jnp.float32)], 0
        )
        high = products.astype(jnp.bfloat16)
        low = (products - high.astype(jnp.float32)).astype(jnp.bfloat16)
        number = lax.broadcasted_iota(jnp.int32, (LANES, ids_out.shape[1]), 0)
        member = (number == ids_out[...]).astype(jnp.float32).astype(jnp.bfloat16)
        sums = transposed_dot(jnp.concatenate([high, low], 0), member)
        rows = stacked.shape[0]
        sums = sums[:rows] + sums[rows:]
        squares, crosses = sums[: rows // 2], sums[rows // 2 :]
        stats_mine[...] = jnp.where(core == 0, squares, crosses)
        theirs[theirs.shape[0] - 1] = jnp.concatenate([jnp.where(core == 0, crosses, squares)] * 2, 0)

    multiply_half(stacked, copies, held, theirs, sum_groups)


def margins_mine_kernel(stacked, labels_ref, a_ref, mine, targets, held, labels_sem, a_sems):
    me = lax.axis_index("feat")
    core, chip = lax.rem(me, 2), lax.div(me, 2)
    copies = start_half(a_ref, core, held, a_sems)
    share = targets.shape[1]
    spot = pl.multiple_of(core * held.shape[1] + chip * share, LANES)
    labels_copy = pltpu.make_async_copy(labels_ref.at[:, pl.ds(spot, share)], targets, labels_sem)
    labels_copy.start()
    multiply_half(stacked[...], copies, held, mine)
    labels_copy.wait()


def weighted_kernel(arrived, targets, copies, totals):
    rows = copies.shape[1]
    probes = rows // 2
    summed = jnp.sum(arrived[...].astype(jnp.float32), 0)
    margins, split_stats = summed[:rows], summed[rows:]
    totals[...] = split_stats[:, :GROUPS] + split_stats[:, GROUPS:]
    likely = 1.0 / (1.0 + jnp.exp(-margins[:probes]))
    weighted = jnp.concatenate(
        [likely - targets[...].astype(jnp.float32), likely * (1.0 - likely) * margins[probes:]], 0
    ).astype(jnp.bfloat16)
    copies[...] = jnp.broadcast_to(weighted[None], copies.shape)


def penalty_kernel(totals_mine, totals_theirs, stacked, ids, out):
    core = lax.rem(lax.axis_index("feat"), 2)
    squares = jnp.where(core == 0, totals_mine[...], totals_theirs[...])
    crosses = jnp.where(core == 0, totals_theirs[...], totals_mine[...])
    probes = squares.shape[0]
    number = lax.broadcasted_iota(jnp.int32, (GROUPS, ids.shape[1]), 0)
    member = (number == ids[...]).astype(jnp.float32)
    group_norm = jnp.sqrt(squares + DELTA * DELTA)
    spread = jnp.dot(
        jnp.concatenate([group_norm, crosses], 0),
        member,
        precision=lax.Precision.HIGHEST,
        preferred_element_type=jnp.float32,
    )
    scale, cross = spread[:probes], spread[probes:]
    wide = stacked[...].astype(jnp.float32)
    weights, direction = wide[:probes], wide[probes:]
    out[:probes] = LAMBDA_WEIGHT * weights / scale
    out[probes:] = LAMBDA_WEIGHT * (
        direction / scale - weights * cross / (scale * scale * scale)
    )


def flatten(weighted, flat):
    for k in range(weighted.shape[0]):
        flat[:, k * LANES : (k + 1) * LANES] = weighted[k]


def fit_kernel(weighted, activations, base, out, flat):
    flatten(weighted, flat)
    out[...] = base[...] + transposed_dot(flat[...], activations[...])


def local(activations, labels, probe_weights, direction, group_ids):
    probes, width = probe_weights.shape
    rows = 2 * probes
    tokens = activations.shape[0]
    half = tokens // 2
    planes = lax.axis_size("tok")
    devices = lax.axis_size("feat")
    chips = devices // 2
    share = half // chips
    by_core = [[2 * i + side for i in range(chips)] for side in range(2)]
    swap = [(i, i ^ 1) for i in range(devices)]
    f32, bf16 = jnp.float32, jnp.bfloat16
    vmem, hbm = pl.BlockSpec(memory_space=pltpu.VMEM), pl.BlockSpec(memory_space=pltpu.HBM)
    held = pltpu.VMEM((width, half), bf16)
    half_cost = pl.CostEstimate(
        flops=2 * rows * width * half, bytes_accessed=2 * width * half, transcendentals=0
    )

    def stay(value):
        return pltpu.with_memory_space_constraint(value, pltpu.HBM)

    by_neuron = stay(activations.T)
    theirs, stats_mine, stacked, ids, a_theirs = pl.pallas_call(
        margins_theirs_kernel,
        out_shape=[
            jax.ShapeDtypeStruct((chips + 1, rows, share), f32),
            jax.ShapeDtypeStruct((probes, LANES), f32),
            jax.ShapeDtypeStruct((rows, width), bf16),
            jax.ShapeDtypeStruct((1, width), jnp.int32),
            held,
        ],
        in_specs=[hbm] * 4,
        out_specs=[vmem] * 5,
        scratch_shapes=[
            pltpu.VMEM((probes, width), bf16),
            pltpu.VMEM((probes, width), bf16),
            pltpu.SemaphoreType.DMA((3,)),
            pltpu.SemaphoreType.DMA((PIECES,)),
        ],
        compiler_params=pltpu.CompilerParams(vmem_limit_bytes=16 << 20),
        cost_estimate=half_cost,
        name="margins_theirs",
    )(stay(probe_weights), stay(direction), stay(group_ids[None, :]), by_neuron)
    from_pair = lax.ppermute(theirs, "feat", swap)
    mine, targets, a_mine = pl.pallas_call(
        margins_mine_kernel,
        out_shape=[
            jax.ShapeDtypeStruct((chips, rows, share), f32),
            jax.ShapeDtypeStruct((probes, share), jnp.int32),
            held,
        ],
        in_specs=[vmem, hbm, hbm],
        out_specs=[vmem] * 3,
        scratch_shapes=[pltpu.SemaphoreType.DMA, pltpu.SemaphoreType.DMA((PIECES,))],
        compiler_params=pltpu.CompilerParams(vmem_limit_bytes=16 << 20),
        cost_estimate=half_cost,
        name="margins_mine",
    )(stacked, stay(labels), by_neuron)
    stats = (stats_mine + from_pair[chips, :probes])[:, :GROUPS]
    high = lax.reduce_precision(stats, 8, 7)
    split_stats = jnp.concatenate([high, stats - high], 1).astype(bf16)
    pair_sum = (mine + from_pair[:chips]).astype(bf16)
    outgoing = jnp.concatenate(
        [pair_sum, jnp.broadcast_to(split_stats[None], (chips, probes, 2 * GROUPS))], 1
    )
    arrived = lax.all_to_all(outgoing, "feat", 0, 0, axis_index_groups=by_core)
    copies, totals_mine = pl.pallas_call(
        weighted_kernel,
        out_shape=[
            jax.ShapeDtypeStruct((chips, rows, share), bf16),
            jax.ShapeDtypeStruct((probes, GROUPS), f32),
        ],
        in_specs=[vmem] * 2,
        out_specs=[vmem] * 2,
        compiler_params=pltpu.CompilerParams(vmem_limit_bytes=4 << 20),
        name="weighted",
    )(arrived, targets)
    weighted_mine = lax.all_to_all(copies, "feat", 0, 0, axis_index_groups=by_core)
    weighted_theirs = lax.ppermute(weighted_mine, "feat", swap)


    def fit(name, weighted, activations, base):
        return pl.pallas_call(
            fit_kernel,
            out_shape=jax.ShapeDtypeStruct((rows, width), f32),
            in_specs=[vmem] * 3,
            out_specs=vmem,
            scratch_shapes=[pltpu.VMEM((rows, half), bf16)],
            compiler_params=pltpu.CompilerParams(vmem_limit_bytes=8 << 20),
            cost_estimate=half_cost,
            name=name,
        )(weighted, pltpu.with_memory_space_constraint(activations, pltpu.VMEM), base)

    fit_mine = fit("fit_mine", weighted_mine, a_mine, jnp.zeros((rows, width), f32))
    local_fit = fit("fit_theirs", weighted_theirs, a_theirs, fit_mine)
    local_fit, totals_mine = lax.optimization_barrier((local_fit, totals_mine))
    one, two, three = (
        lax.ppermute(local_fit, "tok", [(i, (i + hop) % planes) for i in range(planes)])
        for hop in (1, 2, 3)
    )
    fitted = (one + three) + (local_fit + two)
    fitted = fitted / math.sqrt(tokens * planes)

    totals_theirs = lax.ppermute(totals_mine, "feat", swap)
    penalty = pl.pallas_call(
        penalty_kernel,
        out_shape=jax.ShapeDtypeStruct((rows, width), f32),
        in_specs=[vmem] * 4,
        out_specs=vmem,
        compiler_params=pltpu.CompilerParams(vmem_limit_bytes=4 << 20),
        name="penalty",
    )(totals_mine, totals_theirs, stacked, ids)
    gradient = fitted[:probes] + penalty[:probes]
    hess_vec = fitted[probes:] + penalty[probes:]
    return (gradient, hess_vec)


def solution(mesh):
    return jax.shard_map(
        local,
        mesh=mesh,
        in_specs=(P("tok", "feat"), P(None, "tok"), P(None, "feat"), P(None, "feat"), P("feat")),
        out_specs=(P(None, "feat"), P(None, "feat")),
        check_vma=False,
    )
```

```python
import math

import jax
import jax.numpy as jnp
from jax import lax
from jax.experimental import pallas as pl
from jax.experimental.pallas import tpu as pltpu
from jax.sharding import PartitionSpec as P

GROUPS = 64


DELTA = 0.05
LAMBDA_WEIGHT = 8.0

LANES = 128
PIECES = 4
AHEAD = 2


def transposed_dot(left, right, precision=None):
    return lax.dot_general(
        left,
        right,
        (((1,), (1,)), ((), ())),
        precision=precision,
        preferred_element_type=jnp.float32,
    )


def start_copies(a_ref, first, held, sems):
    pieces = sems.shape[0]
    piece = held.shape[1] // pieces
    copies = []
    for i in range(pieces):
        start = pl.multiple_of(first + i * piece, LANES)
        copy = pltpu.make_async_copy(
            a_ref.at[:, pl.ds(start, piece)], held.at[:, pl.ds(i * piece, piece)], sems.at[i]
        )
        copy.start(priority=1)
        copies.append(copy)
    return copies


def multiply(stacked, copies, held, out, skip=0, meanwhile=None):
    piece = held.shape[1] // len(copies)
    per_piece = piece // LANES
    for i, copy in enumerate(copies):
        if i == 1 and meanwhile is not None:
            meanwhile()
        if copy is not None:
            copy.wait()
        product = jnp.dot(
            stacked, held[:, i * piece : (i + 1) * piece], preferred_element_type=jnp.float32
        )
        for k in range(per_piece):
            out[skip + i * per_piece + k] = product[:, k * LANES : (k + 1) * LANES]


def margins_theirs_kernel(
    w_ref, d_ref, g_ref, a_ref,
    theirs, stats_mine, stacked_out, ids_out, held, ahead,
    w, d, small_sems, a_sems, ahead_sems,
):
    core = lax.rem(lax.axis_index("feat"), 2)
    small = [
        pltpu.make_async_copy(source, target, small_sems.at[i])
        for i, (source, target) in enumerate(((w_ref, w), (d_ref, d), (g_ref, ids_out)))
    ]
    for copy in small:
        copy.start()
    half = held.shape[1]
    copies = start_copies(a_ref, (1 - core) * half, held, a_sems)
    ahead_copies = start_copies(a_ref, core * half, ahead, ahead_sems)
    for copy in small:
        copy.wait()
    stacked = jnp.concatenate([w[...], d[...]], 0)
    stacked_out[...] = stacked

    def sum_groups():
        wide_weights = w[...].astype(jnp.float32)
        products = jnp.concatenate(
            [wide_weights * wide_weights, wide_weights * d[...].astype(jnp.float32)], 0
        )
        high = products.astype(jnp.bfloat16)
        low = (products - high.astype(jnp.float32)).astype(jnp.bfloat16)
        number = lax.broadcasted_iota(jnp.int32, (LANES, ids_out.shape[1]), 0)
        member = (number == ids_out[...]).astype(jnp.float32).astype(jnp.bfloat16)
        sums = transposed_dot(jnp.concatenate([high, low], 0), member)
        rows = stacked.shape[0]
        sums = sums[:rows] + sums[rows:]
        squares, crosses = sums[: rows // 2], sums[rows // 2 :]
        stats_mine[...] = jnp.where(core == 0, squares, crosses)
        theirs[theirs.shape[0] - 1] = jnp.concatenate([jnp.where(core == 0, crosses, squares)] * 2, 0)

    multiply(stacked, copies, held, theirs, meanwhile=sum_groups)
    for copy in ahead_copies:
        copy.wait()


def margins_mine_kernel(
    stacked, labels_ref, a_ref, ahead, mine, targets, held, labels_sem, a_sems
):
    me = lax.axis_index("feat")
    core, chip = lax.rem(me, 2), lax.div(me, 2)
    done, rest = ahead.shape[1], held.shape[1]
    copies = start_copies(a_ref, core * (done + rest) + done, held, a_sems)
    share = targets.shape[1]
    spot = pl.multiple_of(core * (done + rest) + chip * share, LANES)
    labels_copy = pltpu.make_async_copy(labels_ref.at[:, pl.ds(spot, share)], targets, labels_sem)
    labels_copy.start()
    multiply(stacked[...], [None] * AHEAD, ahead, mine)
    multiply(stacked[...], copies, held, mine, done // LANES)
    labels_copy.wait()


def weighted_kernel(arrived, targets, copies, totals):
    rows = copies.shape[1]
    probes = rows // 2
    summed = jnp.sum(arrived[...].astype(jnp.float32), 0)
    margins, split_stats = summed[:rows], summed[rows:]
    totals[...] = split_stats[:, :GROUPS] + split_stats[:, GROUPS:]
    likely = 1.0 / (1.0 + jnp.exp(-margins[:probes]))
    weighted = jnp.concatenate(
        [likely - targets[...].astype(jnp.float32), likely * (1.0 - likely) * margins[probes:]], 0
    ).astype(jnp.bfloat16)
    copies[...] = jnp.broadcast_to(weighted[None], copies.shape)


def penalty_kernel(totals_mine, totals_theirs, stacked, ids, out):
    core = lax.rem(lax.axis_index("feat"), 2)
    squares = jnp.where(core == 0, totals_mine[...], totals_theirs[...])
    crosses = jnp.where(core == 0, totals_theirs[...], totals_mine[...])
    probes = squares.shape[0]
    number = lax.broadcasted_iota(jnp.int32, (GROUPS, ids.shape[1]), 0)
    member = (number == ids[...]).astype(jnp.float32)
    group_norm = jnp.sqrt(squares + DELTA * DELTA)
    spread = jnp.dot(
        jnp.concatenate([group_norm, crosses], 0),
        member,
        precision=lax.Precision.HIGHEST,
        preferred_element_type=jnp.float32,
    )
    scale, cross = spread[:probes], spread[probes:]
    wide = stacked[...].astype(jnp.float32)
    weights, direction = wide[:probes], wide[probes:]
    out[:probes] = LAMBDA_WEIGHT * weights / scale
    out[probes:] = LAMBDA_WEIGHT * (
        direction / scale - weights * cross / (scale * scale * scale)
    )


def flatten(weighted, flat):
    for k in range(weighted.shape[0]):
        flat[:, k * LANES : (k + 1) * LANES] = weighted[k]


def fit_kernel(weighted, base, *refs):
    parts, out, flat = refs[:-2], refs[-2], refs[-1]
    flatten(weighted, flat)
    total = base[...]
    start = 0
    for activations in parts:
        end = start + activations.shape[1]
        total = total + transposed_dot(flat[:, start:end], activations[...])
        start = end
    out[...] = total


def local(activations, labels, probe_weights, direction, group_ids):
    probes, width = probe_weights.shape
    rows = 2 * probes
    tokens = activations.shape[0]
    half = tokens // 2
    planes = lax.axis_size("tok")
    devices = lax.axis_size("feat")
    chips = devices // 2
    share = half // chips
    by_core = [[2 * i + side for i in range(chips)] for side in range(2)]
    swap = [(i, i ^ 1) for i in range(devices)]
    f32, bf16 = jnp.float32, jnp.bfloat16
    vmem, hbm = pl.BlockSpec(memory_space=pltpu.VMEM), pl.BlockSpec(memory_space=pltpu.HBM)
    piece = half // PIECES
    held, ahead, rest = (
        pltpu.VMEM((width, pieces * piece), bf16) for pieces in (PIECES, AHEAD, PIECES - AHEAD)
    )
    half_cost = pl.CostEstimate(
        flops=2 * rows * width * half, bytes_accessed=2 * width * half, transcendentals=0
    )

    def in_vmem(value):
        return pltpu.with_memory_space_constraint(value, pltpu.VMEM)

    def stay(value):
        return pltpu.with_memory_space_constraint(value, pltpu.HBM)

    by_neuron = stay(activations.T)
    theirs, stats_mine, stacked, ids, a_theirs, a_ahead = pl.pallas_call(
        margins_theirs_kernel,
        out_shape=[
            jax.ShapeDtypeStruct((chips + 1, rows, share), f32),
            jax.ShapeDtypeStruct((probes, LANES), f32),
            jax.ShapeDtypeStruct((rows, width), bf16),
            jax.ShapeDtypeStruct((1, width), jnp.int32),
            held,
            ahead,
        ],
        in_specs=[hbm] * 4,
        out_specs=[vmem] * 6,
        scratch_shapes=[
            pltpu.VMEM((probes, width), bf16),
            pltpu.VMEM((probes, width), bf16),
            pltpu.SemaphoreType.DMA((3,)),
            pltpu.SemaphoreType.DMA((PIECES,)),
            pltpu.SemaphoreType.DMA((AHEAD,)),
        ],
        compiler_params=pltpu.CompilerParams(vmem_limit_bytes=16 << 20),
        cost_estimate=half_cost,
        name="margins_theirs",
    )(stay(probe_weights), stay(direction), stay(group_ids[None, :]), by_neuron)
    from_pair = lax.ppermute(theirs, "feat", swap)
    mine, targets, a_mine = pl.pallas_call(
        margins_mine_kernel,
        out_shape=[
            jax.ShapeDtypeStruct((chips, rows, share), f32),
            jax.ShapeDtypeStruct((probes, share), jnp.int32),
            rest,
        ],
        in_specs=[vmem, hbm, hbm, vmem],
        out_specs=[vmem] * 3,
        scratch_shapes=[pltpu.SemaphoreType.DMA, pltpu.SemaphoreType.DMA((PIECES - AHEAD,))],
        compiler_params=pltpu.CompilerParams(vmem_limit_bytes=16 << 20),
        cost_estimate=half_cost,
        name="margins_mine",
    )(stacked, stay(labels), by_neuron, in_vmem(a_ahead))
    stats = (stats_mine + from_pair[chips, :probes])[:, :GROUPS]
    high = lax.reduce_precision(stats, 8, 7)
    split_stats = jnp.concatenate([high, stats - high], 1).astype(bf16)
    pair_sum = (mine + from_pair[:chips]).astype(bf16)
    outgoing = jnp.concatenate(
        [pair_sum, jnp.broadcast_to(split_stats[None], (chips, probes, 2 * GROUPS))], 1
    )
    arrived = lax.all_to_all(outgoing, "feat", 0, 0, axis_index_groups=by_core)
    copies, totals_mine = pl.pallas_call(
        weighted_kernel,
        out_shape=[
            jax.ShapeDtypeStruct((chips, rows, share), bf16),
            jax.ShapeDtypeStruct((probes, GROUPS), f32),
        ],
        in_specs=[vmem] * 2,
        out_specs=[vmem] * 2,
        compiler_params=pltpu.CompilerParams(vmem_limit_bytes=4 << 20),
        name="weighted",
    )(arrived, targets)
    weighted_mine = lax.all_to_all(copies, "feat", 0, 0, axis_index_groups=by_core)
    weighted_theirs = lax.ppermute(weighted_mine, "feat", swap)


    def fit(name, weighted, base, *parts):
        return pl.pallas_call(
            fit_kernel,
            out_shape=jax.ShapeDtypeStruct((rows, width), f32),
            in_specs=[vmem] * (2 + len(parts)),
            out_specs=vmem,
            scratch_shapes=[pltpu.VMEM((rows, half), bf16)],
            compiler_params=pltpu.CompilerParams(vmem_limit_bytes=8 << 20),
            cost_estimate=half_cost,
            name=name,
        )(weighted, base, *map(in_vmem, parts))

    fit_mine = fit("fit_mine", weighted_mine, jnp.zeros((rows, width), f32), a_ahead, a_mine)
    local_fit = fit("fit_theirs", weighted_theirs, fit_mine, a_theirs)
    local_fit, totals_mine = lax.optimization_barrier((local_fit, totals_mine))
    one, two, three = (
        lax.ppermute(local_fit, "tok", [(i, (i + hop) % planes) for i in range(planes)])
        for hop in (1, 2, 3)
    )
    fitted = (local_fit + two) + (one + three)
    fitted = fitted / math.sqrt(tokens * planes)

    totals_theirs = lax.ppermute(totals_mine, "feat", swap)
    penalty = pl.pallas_call(
        penalty_kernel,
        out_shape=jax.ShapeDtypeStruct((rows, width), f32),
        in_specs=[vmem] * 4,
        out_specs=vmem,
        compiler_params=pltpu.CompilerParams(vmem_limit_bytes=4 << 20),
        name="penalty",
    )(totals_mine, totals_theirs, stacked, ids)
    gradient = fitted[:probes] + penalty[:probes]
    hess_vec = fitted[probes:] + penalty[probes:]
    return (gradient, hess_vec)


def solution(mesh):
    return jax.shard_map(
        local,
        mesh=mesh,
        in_specs=(P("tok", "feat"), P(None, "tok"), P(None, "feat"), P(None, "feat"), P("feat")),
        out_specs=(P(None, "feat"), P(None, "feat")),
        check_vma=False,
    )
```

```python
import math

import jax
import jax.numpy as jnp
from jax import lax
from jax.experimental import pallas as pl
from jax.experimental.pallas import tpu as pltpu
from jax.sharding import PartitionSpec as P

GROUPS = 64


DELTA = 0.05
LAMBDA_WEIGHT = 8.0

LANES = 128
PIECES = 4
AHEAD = 2


def transposed_dot(left, right, precision=None):
    return lax.dot_general(
        left,
        right,
        (((1,), (1,)), ((), ())),
        precision=precision,
        preferred_element_type=jnp.float32,
    )


def start_copies(a_ref, first, held, sems):
    pieces = sems.shape[0]
    piece = held.shape[1] // pieces
    copies = []
    for i in range(pieces):
        start = pl.multiple_of(first + i * piece, LANES)
        copy = pltpu.make_async_copy(
            a_ref.at[:, pl.ds(start, piece)], held.at[:, pl.ds(i * piece, piece)], sems.at[i]
        )
        copy.start(priority=1)
        copies.append(copy)
    return copies


def multiply(stacked, copies, held, out, skip=0, meanwhile=None):
    piece = held.shape[1] // len(copies)
    per_piece = piece // LANES
    for i, copy in enumerate(copies):
        if i == 1 and meanwhile is not None:
            meanwhile()
        if copy is not None:
            copy.wait()
        product = jnp.dot(
            stacked, held[:, i * piece : (i + 1) * piece], preferred_element_type=jnp.float32
        )
        for k in range(per_piece):
            out[skip + i * per_piece + k] = product[:, k * LANES : (k + 1) * LANES]


def margins_theirs_kernel(
    w_ref, d_ref, g_ref, a_ref,
    theirs, stats_mine, stacked_out, ids_out, held, ahead,
    w, d, small_sems, a_sems, ahead_sems,
):
    core = lax.rem(lax.axis_index("feat"), 2)
    small = [
        pltpu.make_async_copy(source, target, small_sems.at[i])
        for i, (source, target) in enumerate(((w_ref, w), (d_ref, d), (g_ref, ids_out)))
    ]
    for copy in small:
        copy.start()
    half = held.shape[1]
    copies = start_copies(a_ref, (1 - core) * half, held, a_sems)
    ahead_copies = start_copies(a_ref, core * half, ahead, ahead_sems)
    for copy in small:
        copy.wait()
    stacked = jnp.concatenate([w[...], d[...]], 0)
    stacked_out[...] = stacked

    def sum_groups():
        wide_weights = w[...].astype(jnp.float32)
        products = jnp.concatenate(
            [wide_weights * wide_weights, wide_weights * d[...].astype(jnp.float32)], 0
        )
        high = products.astype(jnp.bfloat16)
        low = (products - high.astype(jnp.float32)).astype(jnp.bfloat16)
        number = lax.broadcasted_iota(jnp.int32, (LANES, ids_out.shape[1]), 0)
        member = (number == ids_out[...]).astype(jnp.float32).astype(jnp.bfloat16)
        sums = transposed_dot(jnp.concatenate([high, low], 0), member)
        rows = stacked.shape[0]
        sums = sums[:rows] + sums[rows:]
        squares, crosses = sums[: rows // 2], sums[rows // 2 :]
        stats_mine[...] = jnp.where(core == 0, squares, crosses)
        theirs[theirs.shape[0] - 1] = jnp.concatenate([jnp.where(core == 0, crosses, squares)] * 2, 0)

    multiply(stacked, copies, held, theirs, meanwhile=sum_groups)
    for copy in ahead_copies:
        copy.wait()


def margins_mine_kernel(
    stacked, labels_ref, a_ref, ahead, mine, targets, held, labels_sem, a_sems
):
    me = lax.axis_index("feat")
    core, chip = lax.rem(me, 2), lax.div(me, 2)
    done, rest = ahead.shape[1], held.shape[1]
    copies = start_copies(a_ref, core * (done + rest) + done, held, a_sems)
    share = targets.shape[1]
    spot = pl.multiple_of(core * (done + rest) + chip * share, LANES)
    labels_copy = pltpu.make_async_copy(labels_ref.at[:, pl.ds(spot, share)], targets, labels_sem)
    labels_copy.start()
    multiply(stacked[...], [None] * AHEAD, ahead, mine)
    multiply(stacked[...], copies, held, mine, done // LANES)
    labels_copy.wait()


def weighted_kernel(arrived, targets, copies, totals):
    rows = copies.shape[1]
    probes = rows // 2
    summed = jnp.sum(arrived[...].astype(jnp.float32), 0)
    margins, split_stats = summed[:rows], summed[rows:]
    totals[...] = split_stats[:, :GROUPS] + split_stats[:, GROUPS:]
    likely = 1.0 / (1.0 + jnp.exp(-margins[:probes]))
    weighted = jnp.concatenate(
        [likely - targets[...].astype(jnp.float32), likely * (1.0 - likely) * margins[probes:]], 0
    ).astype(jnp.bfloat16)
    copies[...] = jnp.broadcast_to(weighted[None], copies.shape)


def penalty_kernel(totals_mine, totals_theirs, stacked, ids, out):
    core = lax.rem(lax.axis_index("feat"), 2)
    squares = jnp.where(core == 0, totals_mine[...], totals_theirs[...])
    crosses = jnp.where(core == 0, totals_theirs[...], totals_mine[...])
    probes = squares.shape[0]
    number = lax.broadcasted_iota(jnp.int32, (GROUPS, ids.shape[1]), 0)
    member = (number == ids[...]).astype(jnp.float32)
    group_norm = jnp.sqrt(squares + DELTA * DELTA)
    spread = jnp.dot(
        jnp.concatenate([group_norm, crosses], 0),
        member,
        precision=lax.Precision.HIGHEST,
        preferred_element_type=jnp.float32,
    )
    scale, cross = spread[:probes], spread[probes:]
    wide = stacked[...].astype(jnp.float32)
    weights, direction = wide[:probes], wide[probes:]
    out[:probes] = LAMBDA_WEIGHT * weights / scale
    out[probes:] = LAMBDA_WEIGHT * (
        direction / scale - weights * cross / (scale * scale * scale)
    )


def flatten(weighted, flat):
    for k in range(weighted.shape[0]):
        flat[:, k * LANES : (k + 1) * LANES] = weighted[k]


def fit_kernel(weighted, base, *refs):
    parts, out, flat = refs[:-2], refs[-2], refs[-1]
    flatten(weighted, flat)
    total = base[...]
    start = 0
    for activations in parts:
        end = start + activations.shape[1]
        total = total + transposed_dot(flat[:, start:end], activations[...])
        start = end
    out[...] = total


def local(activations, labels, probe_weights, direction, group_ids):
    probes, width = probe_weights.shape
    rows = 2 * probes
    tokens = activations.shape[0]
    half = tokens // 2
    planes = lax.axis_size("tok")
    devices = lax.axis_size("feat")
    chips = devices // 2
    share = half // chips
    by_core = [[2 * i + side for i in range(chips)] for side in range(2)]
    swap = [(i, i ^ 1) for i in range(devices)]
    f32, bf16 = jnp.float32, jnp.bfloat16
    vmem, hbm = pl.BlockSpec(memory_space=pltpu.VMEM), pl.BlockSpec(memory_space=pltpu.HBM)
    piece = half // PIECES
    held, ahead, rest = (
        pltpu.VMEM((width, pieces * piece), bf16) for pieces in (PIECES, AHEAD, PIECES - AHEAD)
    )
    half_cost = pl.CostEstimate(
        flops=2 * rows * width * half, bytes_accessed=2 * width * half, transcendentals=0
    )

    def in_vmem(value):
        return pltpu.with_memory_space_constraint(value, pltpu.VMEM)

    def stay(value):
        return pltpu.with_memory_space_constraint(value, pltpu.HBM)

    by_neuron = stay(activations.T)
    theirs, stats_mine, stacked, ids, a_theirs, a_ahead = pl.pallas_call(
        margins_theirs_kernel,
        out_shape=[
            jax.ShapeDtypeStruct((chips + 1, rows, share), f32),
            jax.ShapeDtypeStruct((probes, LANES), f32),
            jax.ShapeDtypeStruct((rows, width), bf16),
            jax.ShapeDtypeStruct((1, width), jnp.int32),
            held,
            ahead,
        ],
        in_specs=[hbm] * 4,
        out_specs=[vmem] * 6,
        scratch_shapes=[
            pltpu.VMEM((probes, width), bf16),
            pltpu.VMEM((probes, width), bf16),
            pltpu.SemaphoreType.DMA((3,)),
            pltpu.SemaphoreType.DMA((PIECES,)),
            pltpu.SemaphoreType.DMA((AHEAD,)),
        ],
        compiler_params=pltpu.CompilerParams(vmem_limit_bytes=16 << 20),
        cost_estimate=half_cost,
        name="margins_theirs",
    )(stay(probe_weights), stay(direction), stay(group_ids[None, :]), by_neuron)
    from_pair = lax.ppermute(theirs, "feat", swap)
    mine, targets, a_mine = pl.pallas_call(
        margins_mine_kernel,
        out_shape=[
            jax.ShapeDtypeStruct((chips, rows, share), f32),
            jax.ShapeDtypeStruct((probes, share), jnp.int32),
            rest,
        ],
        in_specs=[vmem, hbm, hbm, vmem],
        out_specs=[vmem] * 3,
        scratch_shapes=[pltpu.SemaphoreType.DMA, pltpu.SemaphoreType.DMA((PIECES - AHEAD,))],
        compiler_params=pltpu.CompilerParams(vmem_limit_bytes=16 << 20),
        cost_estimate=half_cost,
        name="margins_mine",
    )(stacked, stay(labels), by_neuron, in_vmem(a_ahead))
    stats = (stats_mine + from_pair[chips, :probes])[:, :GROUPS]
    high = lax.reduce_precision(stats, 8, 7)
    split_stats = jnp.concatenate([high, stats - high], 1).astype(bf16)
    pair_sum = (mine + from_pair[:chips]).astype(bf16)
    outgoing = jnp.concatenate(
        [pair_sum, jnp.broadcast_to(split_stats[None], (chips, probes, 2 * GROUPS))], 1
    )
    arrived = lax.all_to_all(outgoing, "feat", 0, 0, axis_index_groups=by_core)
    copies, totals_mine = pl.pallas_call(
        weighted_kernel,
        out_shape=[
            jax.ShapeDtypeStruct((chips, rows, share), bf16),
            jax.ShapeDtypeStruct((probes, GROUPS), f32),
        ],
        in_specs=[vmem] * 2,
        out_specs=[vmem] * 2,
        compiler_params=pltpu.CompilerParams(vmem_limit_bytes=4 << 20),
        name="weighted",
    )(arrived, targets)
    weighted_mine = lax.all_to_all(copies, "feat", 0, 0, axis_index_groups=by_core)
    weighted_theirs = lax.ppermute(weighted_mine, "feat", swap)


    def fit(name, weighted, base, *parts):
        return pl.pallas_call(
            fit_kernel,
            out_shape=jax.ShapeDtypeStruct((rows, width), f32),
            in_specs=[vmem] * (2 + len(parts)),
            out_specs=vmem,
            scratch_shapes=[pltpu.VMEM((rows, half), bf16)],
            compiler_params=pltpu.CompilerParams(vmem_limit_bytes=8 << 20),
            cost_estimate=half_cost,
            name=name,
        )(weighted, base, *map(in_vmem, parts))

    fit_mine = fit("fit_mine", weighted_mine, jnp.zeros((rows, width), f32), a_ahead, a_mine)
    local_fit = fit("fit_theirs", weighted_theirs, fit_mine, a_theirs)
    local_fit, totals_mine = lax.optimization_barrier((local_fit, totals_mine))
    one, two, three = (
        lax.ppermute(local_fit, "tok", [(i, (i + hop) % planes) for i in range(planes)])
        for hop in (1, 2, 3)
    )
    fitted = (one + three) + (local_fit + two)
    fitted = fitted / math.sqrt(tokens * planes)

    totals_theirs = lax.ppermute(totals_mine, "feat", swap)
    penalty = pl.pallas_call(
        penalty_kernel,
        out_shape=jax.ShapeDtypeStruct((rows, width), f32),
        in_specs=[vmem] * 4,
        out_specs=vmem,
        compiler_params=pltpu.CompilerParams(vmem_limit_bytes=4 << 20),
        name="penalty",
    )(totals_mine, totals_theirs, stacked, ids)
    gradient = fitted[:probes] + penalty[:probes]
    hess_vec = fitted[probes:] + penalty[probes:]
    return (gradient, hess_vec)


def solution(mesh):
    return jax.shard_map(
        local,
        mesh=mesh,
        in_specs=(P("tok", "feat"), P(None, "tok"), P(None, "feat"), P(None, "feat"), P("feat")),
        out_specs=(P(None, "feat"), P(None, "feat")),
        check_vma=False,
    )
```
